32 devices in a mesh: parts: 2 (over x), tensor: 8 (over z, y), dp: 2 (over core).
Axes of the slice: x: 2, y: 2, z: 4, core: 2. Of those that a mesh axis runs over, the one named last changes fastest.
Arguments:
- train_inputs: bfloat16 [24, 1024, 28672], P(('parts', 'dp'), None, 'tensor'), parts along dimension 0, may hold values from -6 to 6
- train_outgrads: bfloat16 [24, 1024, 8192], P(('parts', 'dp'), None, 'tensor'), parts along dimension 0, may hold values from -6 to 6
- test_inputs: bfloat16 [8, 1024, 28672], P(('parts', 'dp'), None, 'tensor'), parts along dimension 0, may hold values from -6 to 6
- test_outgrads: bfloat16 [8, 1024, 8192], P(('parts', 'dp'), None, 'tensor'), parts along dimension 0, may hold values from -6 to 6
- train_counts: int32 [24], P(('parts', 'dp')), parts along dimension 0, may hold values from 256 to 1024, as said below
- test_counts: int32 [8], P(('parts', 'dp')), parts along dimension 0, may hold values from 256 to 1024, as said below
- proj_in: bfloat16 [64, 28672], P(None, 'tensor'), may hold values from -0.03125 to 0.03125
- proj_out: bfloat16 [64, 8192], P(None, 'tensor'), may hold values from -0.0625 to 0.0625
- fisher_prior: float32 [8192, 4096], P(('parts', 'tensor')), parts along dimension 0, as said below
Outputs:
- scores: float32 [8, 12], P(('parts', 'dp')), parts along dimension 0
- preconditioned: float32 [8, 4096], P(('parts', 'dp'), 'tensor'), parts along dimension 0
The draws below stay inside these ranges and needn't reach their ends.
There are 2 independent parts, one for each index of `parts`. The reference program is written for one: setup_inputs(seed, part) draws one part's arguments, and reference() takes and returns one part's arrays. A program takes and returns all parts, laid end to end along the dimension named above; an argument that names none is the same for every part. Nothing has to cross between parts.
Inputs may be any that keep to these rules, and one draw needn't show every extreme that they name: `train_counts`: in each aligned block of 6 training sequences one has all 1024 tokens live. `test_counts`: in each aligned block of 2 test sequences one has all 1024 tokens live. `fisher_prior`: symmetric and positive definite.
All inputs are finite; a program needn't handle non-finite values.
Results may differ from the reference program's by a relative error of at most 0.0003.
Values sent between devices are 32-bit elements; how exact they have to be, the bound alone decides.
No kernel may reach another device: no remote copies, remote signals or barrier semaphores. Data moves between devices by JAX's collectives and lax.ppermute only.
A program may use at most 192 MiB of HBM per device.

```python
import math
import jax
import jax.numpy as jnp
from jax import lax

D = 8192
FF = 28672
RANK = 64
LENGTH = 1024
TRAIN_DEV = 6
TEST_DEV = 2
ITERS = 6
TRAIN = 12
TEST = 4


def live_counts(key, total, block):
    first, second = jax.random.split(key)
    counts = jax.random.randint(first, (total,), LENGTH // 4, LENGTH + 1, dtype=jnp.int32)
    blocks = total // block
    chosen = jax.random.randint(second, (blocks,), 0, block, dtype=jnp.int32)
    where = jnp.arange(blocks, dtype=jnp.int32) * block + chosen
    return counts.at[where].set(LENGTH)


def draw_train_counts(key, part):
    key = jax.random.fold_in(key, 3)
    return live_counts(key, TRAIN, TRAIN_DEV)


def draw_test_counts(key, part):
    key = jax.random.fold_in(key, 5)
    return live_counts(key, TEST, TEST_DEV)


def draw_fisher_prior(key, part):
    key = jax.random.fold_in(key, 7)
    first, second = jax.random.split(key)
    order = RANK * RANK
    diagonal = jnp.exp(jax.random.uniform(first, (order,), jnp.float32, 0.0, math.log(10.0)))
    upper = jnp.triu(jax.random.uniform(second, (order, order), jnp.float32, -0.006, 0.006), 1)
    return upper + upper.T + jnp.diag(diagonal)


def steps_of(key, extent, cuts, least, high):
    loudness, own = 1.0, jax.random.fold_in(key, 6)
    for dim, shards_of in cuts:
        heights = jnp.exp(jax.random.uniform(jax.random.fold_in(own, dim), (shards_of,), jnp.float32, least / len(cuts), high / len(cuts)))
        loudness = loudness * jnp.repeat(heights, extent[dim] // shards_of).reshape([-1 if axis == dim else 1 for axis in range(len(extent))])
    return loudness


def bell_draw(rng, extent, spread, most, pieces=(), kind=jnp.bfloat16):
    factor_of = steps_of(rng, extent, pieces, -0.22, 0.18) if pieces else 1.0
    array = jax.random.normal(rng, extent, jnp.float32) * spread * factor_of
    return jnp.minimum(jnp.maximum(array, -most), most).astype(kind)


def setup_inputs(seed: int = 0, part: int = 0) -> dict:
    streams_of = jax.random.split(jax.random.key(seed), 10)
    part_splits = jax.random.split(jax.random.fold_in(streams_of[9], part), 10)
    return {
        "train_inputs": bell_draw(part_splits[0], (TRAIN, LENGTH, FF), 1.0, 6.0, ((0, 2), (2, 8))),
        "train_outgrads": bell_draw(part_splits[1], (TRAIN, LENGTH, D), 1.0, 6.0, ((0, 2), (2, 8))),
        "test_inputs": bell_draw(part_splits[2], (TEST, LENGTH, FF), 1.0, 6.0, ((0, 2), (2, 8))),
        "test_outgrads": bell_draw(part_splits[3], (TEST, LENGTH, D), 1.0, 6.0, ((0, 2), (2, 8))),
        "train_counts": draw_train_counts(jax.random.fold_in(jax.random.fold_in(streams_of[9], part), 71), part),
        "test_counts": draw_test_counts(jax.random.fold_in(jax.random.fold_in(streams_of[9], part), 71), part),
        "proj_in": bell_draw(streams_of[6], (RANK, FF), FF ** -0.5, 0.03125, ((1, 8),)),
        "proj_out": bell_draw(streams_of[7], (RANK, D), D ** -0.5, 0.0625, ((1, 8),)),
        "fisher_prior": draw_fisher_prior(jax.random.fold_in(jax.random.fold_in(streams_of[9], part), 71), part),
    }


def project(data, basis):

    def one(example):
        return lax.dot_general(example, basis, (((1,), (1,)), ((), ())), preferred_element_type=jnp.float32)
    return lax.map(one, data)

def outer_sums(left, right, counts):
    length = left.shape[1]
    live = (jnp.arange(length, dtype=jnp.int32)[None, :] < counts[:, None]).astype(jnp.float32)
    grads = jnp.einsum('etr,ets->ers', left * live[:, :, None], right, precision=lax.Precision.HIGHEST)
    return grads.reshape(counts.shape[0], -1) * (1.0 / math.sqrt(length))

def reference(train_inputs, train_outgrads, test_inputs, test_outgrads, train_counts, test_counts, proj_in, proj_out, fisher_prior):
    high = lax.Precision.HIGHEST
    train_grads = outer_sums(project(train_outgrads, proj_out), project(train_inputs, proj_in), train_counts)
    test_grads = outer_sums(project(test_outgrads, proj_out), project(test_inputs, proj_in), test_counts)
    fisher = fisher_prior + jnp.dot(train_grads.T, train_grads, precision=high) / TRAIN
    solution = jnp.zeros_like(test_grads)
    residue = test_grads
    search = test_grads
    norm_now = lax.optimization_barrier(jnp.sum(residue * residue, axis=1))
    for step in range(ITERS):
        image = jnp.dot(search, fisher.T, precision=high)
        alpha = norm_now / lax.optimization_barrier(jnp.sum(search * image, axis=1))
        solution = solution + alpha[:, None] * search
        residue = residue - alpha[:, None] * image
        norm_next = lax.optimization_barrier(jnp.sum(residue * residue, axis=1))
        search = residue + (norm_next / norm_now)[:, None] * search
        norm_now = norm_next
    scores = jnp.dot(solution, train_grads.T, precision=high) / RANK
    return (scores, solution)
```

```python
import functools
import math

import jax
import jax.numpy as jnp
from jax import lax
from jax.experimental import pallas as pl
from jax.experimental.pallas import tpu as pltpu
from jax.sharding import PartitionSpec as P

RANK = 64
ITERS = 6
LANES = 128
CHUNKS = (256, 256, 256, 256)
TILE = 256
SLOTS = 3

HIGH = lax.Precision.HIGHEST
VMEM = pl.BlockSpec(memory_space=pltpu.VMEM)
SMEM = pl.BlockSpec(memory_space=pltpu.SMEM)
ANY = pl.BlockSpec(memory_space=pl.ANY)


def project(data, basis):
    rows = data.reshape(-1, data.shape[-1])
    return lax.dot_general(
        rows, basis, (((1,), (1,)), ((), ())), preferred_element_type=jnp.float32
    )


def outer_sums(left, right, counts, length):
    examples = counts.shape[0]
    left = left.reshape(examples, length, -1)
    right = right.reshape(examples, length, -1)
    live = (jnp.arange(length, dtype=jnp.int32)[None, :] < counts[:, None]).astype(jnp.float32)
    grads = jnp.einsum("etr,ets->ers", left * live[:, :, None], right, precision=HIGH)
    return grads.reshape(examples, -1) * (1.0 / math.sqrt(length))


def plain(
    train_inputs,
    train_outgrads,
    test_inputs,
    test_outgrads,
    train_counts,
    test_counts,
    proj_in,
    proj_out,
    fisher_prior,
):
    length = train_inputs.shape[1]
    left_train = project(train_outgrads, proj_out)
    right_train = project(train_inputs, proj_in)
    left_test = project(test_outgrads, proj_out)
    right_test = project(test_inputs, proj_in)
    left_train, right_train, left_test, right_test = lax.psum(
        (left_train, right_train, left_test, right_test), "tensor"
    )
    train_grads = outer_sums(left_train, right_train, train_counts, length)
    test_grads = outer_sums(left_test, right_test, test_counts, length)
    every_train = lax.all_gather(train_grads, "dp", axis=0, tiled=True)
    total_train = every_train.shape[0]
    own_rows = fisher_prior.shape[0]
    start = lax.axis_index("tensor") * own_rows
    own_train = lax.dynamic_slice_in_dim(every_train, start, own_rows, 1)
    fisher_rows = fisher_prior + jnp.dot(own_train.T, every_train, precision=HIGH) / total_train
    residue = test_grads
    search = test_grads
    solution = jnp.zeros_like(test_grads)
    norm_now = jnp.sum(test_grads * test_grads, axis=1)
    for step in range(ITERS):
        part = lax.dot_general(search, fisher_rows, (((1,), (1,)), ((), ())), precision=HIGH)
        image = lax.all_gather(part, "tensor", axis=1, tiled=True)
        alpha = norm_now / jnp.sum(search * image, axis=1)
        solution = solution + alpha[:, None] * search
        residue = residue - alpha[:, None] * image
        norm_next = jnp.sum(residue * residue, axis=1)
        search = residue + (norm_next / norm_now)[:, None] * search
        norm_now = norm_next
    scores = jnp.dot(solution, every_train.T, precision=HIGH) / RANK
    return (scores, lax.dynamic_slice_in_dim(solution, start, own_rows, 1))


def project_kernel(
    flip, first, size, tile, train_count, test_count, train_in, train_out, test_in, test_out,
    basis_in, basis_out, out, held_in, held_out, sems,
):
    low = lax.rem(lax.axis_index("tensor"), 2)
    low = 1 - low if flip else low
    each = size // tile
    total = 4 * each
    last = train_in.shape[0] // 2

    def place(k):
        return k // each, first + lax.rem(k, each) * tile

    def live(k):
        i, row = place(k)
        count = jnp.where(
            i < last, train_count[jnp.minimum(2 * i + low, 2 * last - 1)], test_count[low]
        )
        return count > row

    def copies(k, train):
        i, row = place(k)
        slot = lax.rem(k, SLOTS)
        rows = pl.ds(row, tile)
        wide, narrow, e = (train_in, train_out, 2 * i + low) if train else (test_in, test_out, low)
        return (
            pltpu.make_async_copy(wide.at[e, rows], held_in.at[slot], sems.at[slot, 0]),
            pltpu.make_async_copy(narrow.at[e, rows], held_out.at[slot], sems.at[slot, 1]),
        )

    def start(k):
        i, _ = place(k)

        @pl.when(live(k) & (i < last))
        def _():
            for copy in copies(k, True):
                copy.start()

        @pl.when(live(k) & (i == last))
        def _():
            for copy in copies(k, False):
                copy.start()

    for k in range(SLOTS - 1):
        start(jnp.int32(k))

    @pl.loop(0, total)
    def _(k):
        i, row = place(k)
        slot = lax.rem(k, SLOTS)

        @pl.when(k + SLOTS - 1 < total)
        def _():
            start(k + SLOTS - 1)

        there = pl.ds(row - first, tile)

        @pl.when(live(k))
        def _():
            for copy in copies(k, False):
                copy.wait()
            out[i, there, :] = jnp.dot(
                held_out[slot], basis_out[...], preferred_element_type=jnp.float32
            ) + jnp.dot(held_in[slot], basis_in[...], preferred_element_type=jnp.float32)

        @pl.when(jnp.logical_not(live(k)))
        def _():
            out[i, there, :] = jnp.zeros((tile, LANES), jnp.float32)


def project_rows(flip, first, size, tile, operands):
    wide, narrow = operands[2], operands[3]
    return pl.pallas_call(
        functools.partial(project_kernel, flip, first, size, tile),
        out_shape=jax.ShapeDtypeStruct((4, size, LANES), jnp.float32),
        in_specs=[SMEM, SMEM, ANY, ANY, ANY, ANY, VMEM, VMEM],
        out_specs=VMEM,
        scratch_shapes=[
            pltpu.VMEM((SLOTS, tile, wide.shape[2]), wide.dtype),
            pltpu.VMEM((SLOTS, tile, narrow.shape[2]), narrow.dtype),
            pltpu.SemaphoreType.DMA((SLOTS, 2)),
        ],
        compiler_params=pltpu.CompilerParams(vmem_limit_bytes=24 * 2**20),
        cost_estimate=pl.CostEstimate(
            flops=2 * 4 * size * 4608 * 64, bytes_accessed=4 * size * 4608 * 2, transcendentals=0
        ),
        name=f"project_{'send' if flip else 'keep'}_{first}",
    )(*operands)


def gram_kernel(count, rows, out, held):
    live = lax.broadcasted_iota(jnp.int32, rows.shape, 0) < count[0]
    vectors = jnp.where(live, rows[...], 0.0)
    held[...] = lax.dot_general(
        vectors[:, :RANK], vectors[:, RANK:], (((0,), (0,)), ((), ())), precision=HIGH,
        preferred_element_type=jnp.float32,
    ) * (1.0 / math.sqrt(rows.shape[0]))
    half = RANK // 2
    grad = jnp.concatenate(
        [held[pl.ds(0, half, stride=2), :], held[pl.ds(1, half, stride=2), :]], axis=1
    )
    for i in range(out.shape[0]):
        out[i] = grad


def gram(count, rows, n):
    return pl.pallas_call(
        gram_kernel,
        out_shape=jax.ShapeDtypeStruct((n, RANK // 2, LANES), jnp.float32),
        in_specs=[SMEM, VMEM],
        out_specs=VMEM,
        scratch_shapes=[pltpu.VMEM((RANK, RANK), jnp.float32)],
        name="gram",
    )(count, rows)


def pair_sums(x):
    x = jnp.sum(x, axis=-1, keepdims=True)
    upper = lax.broadcasted_iota(jnp.int32, x.shape, x.ndim - 2) < 4
    first = jnp.sum(jnp.where(upper, x, 0.0), axis=-2, keepdims=True)
    second = jnp.sum(jnp.where(upper, 0.0, x), axis=-2, keepdims=True)
    return jnp.where(upper, first, second)


def inner(a, b):
    return pair_sums(jnp.sum(a * b, axis=0))


def weights_of(grads, vector):
    return pair_sums(
        jnp.stack([jnp.sum(grads[i] * vector, axis=0) for i in range(grads.shape[0])])
    )


def fisher_rows(prior, grads, vector, weights, image):
    me = lax.axis_index("tensor")
    ones = jnp.ones((8, LANES), jnp.float32)

    @pl.loop(0, prior.shape[0] // LANES)
    def _(block):
        rows = pl.ds(pl.multiple_of(block * LANES, LANES), LANES)
        sums = [jnp.zeros((LANES, LANES), jnp.float32)] * 2
        for c in range(prior.shape[1] // LANES):
            piece = prior[rows, pl.ds(c * LANES, LANES)]
            for j in range(2):
                sums[j] = sums[j] + piece * vector[c // 4, pl.ds(j * 4 + c % 4, 1), :]
        for j in range(2):
            line = lax.dot_general(
                ones, sums[j], (((1,), (1,)), ((), ())), precision=HIGH,
                preferred_element_type=jnp.float32,
            )
            image[pl.ds(j * 4 + block, 1), :] = line[:1]

    total = grads.shape[0]
    low = weights[0] * grads[0, me]
    for i in range(1, total):
        low = low + weights[i] * grads[i, me]
    image[...] = image[...] + low * (1.0 / total)


def begin_kernel(own, other, prior, grads, search, payload, image):
    me = lax.axis_index("dp")
    per = other.shape[0]
    for i in range(per):
        for s in range(8):
            for half in range(2):
                grads[me * per + i, s, pl.ds(half * 4, 4), :] = own[i, pl.ds(s * 4, 4), :]
                grads[(1 - me) * per + i, s, pl.ds(half * 4, 4), :] = other[i, pl.ds(s * 4, 4), :]
    for j in range(2):
        for s in range(8):
            search[s, pl.ds(j * 4, 4), :] = own[per + j, pl.ds(s * 4, 4), :]
    fisher_rows(prior, grads, search, weights_of(grads, search[...]), image)
    for s in range(8):
        payload[s] = image[...]


def advance(first, images, solution, residue, search, new_solution, new_residue, new_search):
    old = search[...]
    rest = old if first else residue[...]
    image = images[...]
    norm = inner(rest, rest)
    alpha = norm / inner(old, image)
    new_solution[...] = alpha * old if first else solution[...] + alpha * old
    rest = rest - alpha * image
    new_residue[...] = rest
    norm_next = inner(rest, rest)
    new_search[...] = rest + (norm_next / norm) * old
    return norm_next


def step_kernel(
    images, solution, residue, search, grads, prior,
    new_solution, new_residue, new_search, payload, image,
):
    advance(False, images, solution, residue, search, new_solution, new_residue, new_search)
    fisher_rows(prior, grads, new_search, weights_of(grads, new_search[...]), image)
    for s in range(8):
        payload[s] = image[...]


def first_kernel(
    images, search, grads, prior, new_solution, new_residue, new_search, payload, image
):
    advance(True, images, None, None, search, new_solution, new_residue, new_search)
    fisher_rows(prior, grads, new_search, weights_of(grads, new_search[...]), image)
    for s in range(8):
        payload[s] = image[...]


def last_kernel(
    images, solution, residue, search, grads, prior,
    own, payload, values, new_solution, new_residue, new_search, image,
):
    me = lax.axis_index("tensor")
    norm = advance(False, images, solution, residue, search, new_solution, new_residue, new_search)
    weights = weights_of(grads, new_search[...])
    fisher_rows(prior, grads, new_search, weights, image)
    curve = pair_sums(new_search[me] * image[...])
    for s in range(8):
        payload[s] = jnp.broadcast_to(curve, (8, LANES))
    own[0] = new_solution[me]
    own[1] = new_search[me]
    own[2] = jnp.broadcast_to(norm, (8, LANES))
    values[0] = jnp.broadcast_to(weights_of(grads, new_solution[...]), values.shape[1:])
    values[1] = jnp.broadcast_to(weights, values.shape[1:])


def end_kernel(curves, own, values, scores, solution):
    alpha = own[2] / jnp.sum(curves[...], axis=0)
    done = own[0] + alpha * own[1]
    for j in range(2):
        for c in range(4):
            solution[pl.ds(j, 1), pl.ds(c * LANES, LANES)] = done[j * 4 + c : j * 4 + c + 1]
    total = values.shape[1]
    lane = lax.broadcasted_iota(jnp.int32, (8, LANES), 1)
    table = jnp.zeros((8, LANES), jnp.float32)
    for i in range(total):
        table = jnp.where(lane == i, (values[0, i] + alpha * values[1, i]) / RANK, table)
    for j in range(2):
        scores[pl.ds(j, 1), :] = table[j * 4 : j * 4 + 1, :total]


def call(kernel, shapes, operands, scratch=(), limit=16):
    return pl.pallas_call(
        kernel,
        out_shape=[jax.ShapeDtypeStruct(s, jnp.float32) for s in shapes],
        in_specs=[VMEM] * len(operands),
        out_specs=[VMEM] * len(shapes),
        scratch_shapes=[pltpu.VMEM(s, jnp.float32) for s in scratch],
        compiler_params=pltpu.CompilerParams(vmem_limit_bytes=limit * 2**20),
        name=kernel.__name__,
    )(*operands)


def flipped(n, bit):
    return [(i, i ^ bit) for i in range(n)]


def per_device(
    train_inputs,
    train_outgrads,
    test_inputs,
    test_outgrads,
    train_counts,
    test_counts,
    proj_in,
    proj_out,
    fisher_prior,
):
    n = 8
    me = lax.axis_index("tensor")
    near, far = (me >> 1) & 1, me >> 2
    length = train_inputs.shape[1]
    basis_out = jnp.concatenate([proj_out, jnp.zeros_like(proj_out)], 0).T
    basis_in = jnp.concatenate([jnp.zeros_like(proj_in), proj_in], 0).T
    operands = (
        train_counts, test_counts, train_inputs, train_outgrads, test_inputs, test_outgrads,
        basis_in, basis_out,
    )
    firsts = [sum(CHUNKS[:c]) for c in range(len(CHUNKS))]
    arrived = []
    for first, size in zip(firsts, CHUNKS):
        sent = project_rows(True, first, size, min(TILE, size), operands)
        arrived.append(lax.ppermute(sent, "tensor", flipped(n, 1)))
    kept = project_rows(False, 0, length, TILE, operands)
    whole = []
    for first, size, got in zip(firsts, CHUNKS, arrived):
        pair = (kept[:, first : first + size] + got).reshape(2, 2, size, LANES)
        ours = lax.dynamic_index_in_dim(pair, near, 1, False)
        theirs = lax.dynamic_index_in_dim(pair, 1 - near, 1, False)
        quad = ours + lax.ppermute(theirs, "tensor", flipped(n, 2))
        ours = lax.dynamic_index_in_dim(quad, far, 0, False)
        theirs = lax.dynamic_index_in_dim(quad, 1 - far, 0, False)
        whole.append(ours + lax.ppermute(theirs, "tensor", flipped(n, 4)))
    counts = jnp.concatenate([train_counts, test_counts])
    grad = gram(lax.dynamic_slice_in_dim(counts, me, 1), jnp.concatenate(whole), n)
    own = lax.all_to_all(grad, "tensor", 0, 0, tiled=True)
    per = train_inputs.shape[0]
    other = lax.ppermute(own[:per], "dp", flipped(2, 1))
    state = (8, 8, LANES)
    piece = (8, LANES)
    total = 2 * per
    grads, search, payload = call(
        begin_kernel, [(total, 8, 8, LANES), state, state], (own, other, fisher_prior), [piece]
    )
    swap = lambda x: lax.all_to_all(x, "tensor", 0, 0, tiled=True)
    solution, residue, search, payload = call(
        first_kernel, [state] * 4, (swap(payload), search, grads, fisher_prior), [piece]
    )
    for _ in range(ITERS - 3):
        solution, residue, search, payload = call(
            step_kernel,
            [state] * 4,
            (swap(payload), solution, residue, search, grads, fisher_prior),
            [piece],
        )
    ours, payload, values = call(
        last_kernel,
        [(3, 8, LANES), state, (2, total, 8, LANES)],
        (swap(payload), solution, residue, search, grads, fisher_prior),
        [state, state, state, piece],
    )
    return tuple(
        call(
            end_kernel,
            [(2, total), (2, fisher_prior.shape[0])],
            (swap(payload), ours, values),
        )
    )


def solution(mesh):
    in_specs = (
        P(("parts", "dp"), None, "tensor"),
        P(("parts", "dp"), None, "tensor"),
        P(("parts", "dp"), None, "tensor"),
        P(("parts", "dp"), None, "tensor"),
        P(("parts", "dp")),
        P(("parts", "dp")),
        P(None, "tensor"),
        P(None, "tensor"),
        P(("parts", "tensor"), None),
    )
    out_specs = (P(("parts", "dp"), None), P(("parts", "dp"), "tensor"))
    body = per_device if mesh.shape["tensor"] == 8 and mesh.shape["dp"] == 2 else plain
    return jax.shard_map(
        body, mesh=mesh, in_specs=in_specs, out_specs=out_specs, check_vma=False
    )
```

```python
import functools
import math

import jax
import jax.numpy as jnp
from jax import lax
from jax.experimental import pallas as pl
from jax.experimental.pallas import tpu as pltpu
from jax.sharding import PartitionSpec as P

RANK = 64
ITERS = 6
LANES = 128
FLOOR = 256
SLOTS = 3
SMALL = 24 * 2**20

HIGH = lax.Precision.HIGHEST
VMEM = pl.BlockSpec(memory_space=pltpu.VMEM)
SMEM = pl.BlockSpec(memory_space=pltpu.SMEM)
ANY = pl.BlockSpec(memory_space=pl.ANY)


def project(data, basis):
    rows = data.reshape(-1, data.shape[-1])
    return lax.dot_general(
        rows, basis, (((1,), (1,)), ((), ())), preferred_element_type=jnp.float32
    )


def outer_sums(left, right, counts, length):
    examples = counts.shape[0]
    left = left.reshape(examples, length, -1)
    right = right.reshape(examples, length, -1)
    live = (jnp.arange(length, dtype=jnp.int32)[None, :] < counts[:, None]).astype(jnp.float32)
    grads = jnp.einsum("etr,ets->ers", left * live[:, :, None], right, precision=HIGH)
    return grads.reshape(examples, -1) * (1.0 / math.sqrt(length))


def plain(
    train_inputs,
    train_outgrads,
    test_inputs,
    test_outgrads,
    train_counts,
    test_counts,
    proj_in,
    proj_out,
    fisher_prior,
):
    length = train_inputs.shape[1]
    left_train = project(train_outgrads, proj_out)
    right_train = project(train_inputs, proj_in)
    left_test = project(test_outgrads, proj_out)
    right_test = project(test_inputs, proj_in)
    left_train, right_train, left_test, right_test = lax.psum(
        (left_train, right_train, left_test, right_test), "tensor"
    )
    train_grads = outer_sums(left_train, right_train, train_counts, length)
    test_grads = outer_sums(left_test, right_test, test_counts, length)
    every_train = lax.all_gather(train_grads, "dp", axis=0, tiled=True)
    total_train = every_train.shape[0]
    own_rows = fisher_prior.shape[0]
    start = lax.axis_index("tensor") * own_rows
    own_train = lax.dynamic_slice_in_dim(every_train, start, own_rows, 1)
    fisher_rows = fisher_prior + jnp.dot(own_train.T, every_train, precision=HIGH) / total_train
    residue = test_grads
    search = test_grads
    solution = jnp.zeros_like(test_grads)
    norm_now = jnp.sum(test_grads * test_grads, axis=1)
    for step in range(ITERS):
        part = lax.dot_general(search, fisher_rows, (((1,), (1,)), ((), ())), precision=HIGH)
        image = lax.all_gather(part, "tensor", axis=1, tiled=True)
        alpha = norm_now / jnp.sum(search * image, axis=1)
        solution = solution + alpha[:, None] * search
        residue = residue - alpha[:, None] * image
        norm_next = jnp.sum(residue * residue, axis=1)
        search = residue + (norm_next / norm_now)[:, None] * search
        norm_now = norm_next
    scores = jnp.dot(solution, every_train.T, precision=HIGH) / RANK
    return (scores, lax.dynamic_slice_in_dim(solution, start, own_rows, 1))


def project_kernel(
    parts, after, train_count, test_count, train_in, train_out, test_in, test_out,
    basis_in, basis_out, *rest,
):
    outs = rest[after : after + len(parts)]
    held_in, held_out, near_in, near_out, of_train, of_test, sems, more = rest[after + len(parts) :]
    me = lax.rem(lax.axis_index("tensor"), 2)
    last = train_in.shape[0] // 2
    begins = [0]
    for _, _, size, tile in parts:
        begins.append(begins[-1] + 4 * (size // tile))
    dynamic = [max(range(first, first + size, tile)) >= FLOOR for _, first, size, tile in parts]

    def place(part, k):
        flip, first, size, tile = parts[part]
        each = size // tile
        low = 1 - me if flip else me
        step = k - begins[part]
        return step // each, first + lax.rem(step, each) * tile, low

    def live(part, k):
        i, row, low = place(part, k)
        train = of_train[jnp.minimum(2 * i + low, 2 * last - 1)]
        return (jnp.where(i < last, train, of_test[low]) > row) | (k == 0)

    def copies(part, k, train):
        i, row, low = place(part, k)
        tile = parts[part][3]
        slot = lax.rem(k, SLOTS)
        rows, there = pl.ds(row, tile), pl.ds(0, tile)
        wide, narrow, e = (train_in, train_out, 2 * i + low) if train else (test_in, test_out, low)
        return (
            pltpu.make_async_copy(wide.at[e, rows], held_in.at[slot, there], sems.at[slot, 0]),
            pltpu.make_async_copy(narrow.at[e, rows], held_out.at[slot, there], sems.at[slot, 1]),
        )

    def start(k, among):
        for part in among:
            mine = (k >= begins[part]) & (k < begins[part + 1])
            if dynamic[part]:
                mine = mine & live(part, k)
            i, _, _ = place(part, k)

            @pl.when(mine & (i < last))
            def _():
                for copy in copies(part, k, True):
                    copy.start()

            @pl.when(mine & (i == last))
            def _():
                for copy in copies(part, k, False):
                    copy.start()

    bases = (
        pltpu.make_async_copy(basis_in, near_in, more.at[0]),
        pltpu.make_async_copy(basis_out, near_out, more.at[1]),
    )
    lengths = (
        pltpu.make_async_copy(train_count, of_train, more.at[2]),
        pltpu.make_async_copy(test_count, of_test, more.at[3]),
    )
    if any(dynamic):
        for copy in lengths:
            copy.start()
    for copy in copies(0, jnp.int32(0), True):
        copy.start()
    for copy in bases:
        copy.start()
    if any(dynamic):
        for copy in lengths:
            copy.wait()
    for k in range(1, SLOTS - 1):
        start(jnp.int32(k), range(len(parts)))
    for copy in bases:
        copy.wait()

    for part, (flip, first, size, tile) in enumerate(parts):

        @pl.loop(begins[part], begins[part + 1])
        def _(k):
            i, row, _ = place(part, k)
            slot = lax.rem(k, SLOTS)
            start(k + SLOTS - 1, range(part, len(parts)))
            there, whole = pl.ds(row - first, tile), pl.ds(0, tile)

            def make():
                for copy in copies(part, k, False):
                    copy.wait()
                dims = (((1,), (1,)), ((), ()))
                left = lax.dot_general(
                    held_out[slot, whole], near_out[...], dims, preferred_element_type=jnp.float32
                )
                right = lax.dot_general(
                    held_in[slot, whole], near_in[...], dims, preferred_element_type=jnp.float32
                )
                outs[part][i, there, :] = jnp.concatenate([left, right], axis=1)

            if dynamic[part]:
                alive = live(part, k)
                pl.when(alive)(make)

                @pl.when(jnp.logical_not(alive))
                def _():
                    outs[part][i, there, :] = jnp.zeros((tile, LANES), jnp.float32)

            else:
                make()


def in_hbm(arrays):
    return [pltpu.with_memory_space_constraint(x, pltpu.HBM) for x in arrays]


def project_rows(parts, operands, after=()):
    wide, narrow, basis_in, basis_out = operands[2], operands[3], operands[6], operands[7]
    tile = max(part[3] for part in parts)
    rows = 4 * sum(part[2] for part in parts)
    depth = wide.shape[2] + narrow.shape[2]
    return pl.pallas_call(
        functools.partial(project_kernel, parts, len(after)),
        out_shape=[pltpu.VMEM((4, part[2], LANES), jnp.float32) for part in parts],
        in_specs=[ANY] * (len(operands) + len(after)),
        out_specs=[VMEM] * len(parts),
        scratch_shapes=[
            pltpu.VMEM((SLOTS, tile, wide.shape[2]), wide.dtype),
            pltpu.VMEM((SLOTS, tile, narrow.shape[2]), narrow.dtype),
            pltpu.VMEM(basis_in.shape, basis_in.dtype),
            pltpu.VMEM(basis_out.shape, basis_out.dtype),
            pltpu.SMEM(operands[0].shape, jnp.int32),
            pltpu.SMEM(operands[1].shape, jnp.int32),
            pltpu.SemaphoreType.DMA((SLOTS, 2)),
            pltpu.SemaphoreType.DMA((4,)),
        ],
        compiler_params=pltpu.CompilerParams(vmem_limit_bytes=SMALL),
        cost_estimate=pl.CostEstimate(
            flops=2 * rows * depth * RANK, bytes_accessed=rows * depth * 2, transcendentals=0
        ),
        name="project_" + "_".join(f"{'send' if p[0] else 'keep'}{p[1]}" for p in parts),
    )(*in_hbm(operands), *after)


def halve_kernel(offset, bit, pieces, kept, *rest):
    got, (theirs, ours) = rest[:pieces], rest[-2:]
    mine = (lax.axis_index("tensor") >> bit) & 1
    groups = theirs.shape[0]
    at = 0
    for piece in got:
        rows = piece.shape[1]
        here, there = pl.ds(offset + at, rows), pl.ds(at, rows)
        for h in range(groups):
            give = 2 * h + 1 - mine if bit == 1 else 1 - mine
            take = 2 * h + mine if bit == 1 else mine
            theirs[h, there, :] = kept[give, here, :] + piece[give, :, :]
            ours[h, there, :] = kept[take, here, :] + piece[take, :, :]
        at += rows


def halve(offset, bit, kept, got, after=()):
    rows = sum(piece.shape[1] for piece in got)
    shape = pltpu.VMEM((kept.shape[0] // 2, rows, LANES), jnp.float32)
    return pl.pallas_call(
        functools.partial(halve_kernel, offset, bit, len(got)),
        out_shape=[shape, shape],
        in_specs=[VMEM] * (1 + len(got)) + [ANY] * len(after),
        out_specs=[VMEM, VMEM],
        compiler_params=pltpu.CompilerParams(vmem_limit_bytes=SMALL),
        name=f"halve{bit}",
    )(kept, *got, *after)


def gram_kernel(first, pieces, length, final, train_count, test_count, *rest):
    ours, got = rest[:pieces], rest[pieces : 2 * pieces]
    rest = rest[2 * pieces :]
    if final:
        before, out, held, of_train, of_test, sems = rest
    else:
        prior, out, near, of_train, of_test, sems, more = rest
        fetch = pltpu.make_async_copy(prior, near, more)
        fetch.start()
    me = lax.axis_index("tensor")
    train = train_count.shape[0]
    lengths = (
        pltpu.make_async_copy(train_count, of_train, sems.at[0]),
        pltpu.make_async_copy(test_count, of_test, sems.at[1]),
    )
    for copy in lengths:
        copy.start()
    for copy in lengths:
        copy.wait()
    count = jnp.where(
        me < train, of_train[jnp.minimum(me, train - 1)], of_test[jnp.maximum(me - train, 0)]
    )
    total = before[...] if final else jnp.zeros((RANK, RANK), jnp.float32)
    for a, b in zip(ours, got):
        rows = a[0] + b[0]
        live = lax.broadcasted_iota(jnp.int32, rows.shape, 0) + first < count
        rows = jnp.where(live, rows, 0.0)
        total = total + lax.dot_general(
            rows[:, :RANK], rows[:, RANK:], (((0,), (0,)), ((), ())), precision=HIGH,
            preferred_element_type=jnp.float32,
        )
        first += rows.shape[0]
    if not final:
        out[...] = total
        fetch.wait()
        return
    held[...] = total * (1.0 / math.sqrt(length))
    half = RANK // 2
    grad = jnp.concatenate(
        [held[pl.ds(0, half, stride=2), :], held[pl.ds(1, half, stride=2), :]], axis=1
    )
    for i in range(out.shape[0]):
        out[i] = grad


def gram(first, length, counts, ours, got, prior=None, before=None):
    final = before is not None
    square = jax.ShapeDtypeStruct((RANK, RANK), jnp.float32)
    scratch = [pltpu.SMEM(c.shape, jnp.int32) for c in counts] + [pltpu.SemaphoreType.DMA((2,))]
    if final:
        out_shape = jax.ShapeDtypeStruct((8, RANK // 2, LANES), jnp.float32)
        scratch = [pltpu.VMEM((RANK, RANK), jnp.float32)] + scratch
    else:
        out_shape = [square, pltpu.VMEM(prior.shape, prior.dtype)]
        counts, (prior,) = in_hbm(counts), in_hbm([prior])
        scratch = scratch + [pltpu.SemaphoreType.DMA]
    return pl.pallas_call(
        functools.partial(gram_kernel, first, len(ours), length, final),
        out_shape=out_shape,
        in_specs=[ANY, ANY] + [VMEM] * (2 * len(ours)) + [VMEM if final else ANY],
        out_specs=VMEM if final else [VMEM, VMEM],
        scratch_shapes=scratch,
        compiler_params=pltpu.CompilerParams(vmem_limit_bytes=SMALL),
        name="gram_end" if final else "gram_begin",
    )(*counts, *ours, *got, before if final else prior)


def pair_sums(x):
    x = jnp.sum(x, axis=-1, keepdims=True)
    upper = lax.broadcasted_iota(jnp.int32, x.shape, x.ndim - 2) < 4
    first = jnp.sum(jnp.where(upper, x, 0.0), axis=-2, keepdims=True)
    second = jnp.sum(jnp.where(upper, 0.0, x), axis=-2, keepdims=True)
    return jnp.where(upper, first, second)


def inner(a, b):
    return pair_sums(jnp.sum(a * b, axis=0))


def weights_of(grads, vector):
    return pair_sums(
        jnp.stack([jnp.sum(grads[i] * vector, axis=0) for i in range(grads.shape[0])])
    )


def fisher_rows(prior, grads, vector, weights, image):
    me = lax.axis_index("tensor")
    ones = jnp.ones((8, LANES), jnp.float32)

    @pl.loop(0, prior.shape[0] // LANES)
    def _(block):
        rows = pl.ds(pl.multiple_of(block * LANES, LANES), LANES)
        sums = [jnp.zeros((LANES, LANES), jnp.float32)] * 2
        for c in range(prior.shape[1] // LANES):
            piece = prior[rows, pl.ds(c * LANES, LANES)]
            for j in range(2):
                sums[j] = sums[j] + piece * vector[c // 4, pl.ds(j * 4 + c % 4, 1), :]
        for j in range(2):
            line = lax.dot_general(
                ones, sums[j], (((1,), (1,)), ((), ())), precision=HIGH,
                preferred_element_type=jnp.float32,
            )
            image[pl.ds(j * 4 + block, 1), :] = line[:1]

    total = grads.shape[0]
    low = weights[0] * grads[0, me]
    for i in range(1, total):
        low = low + weights[i] * grads[i, me]
    image[...] = image[...] + low * (1.0 / total)


def begin_kernel(own, other, prior, grads, search, payload, image):
    me = lax.axis_index("dp")
    per = other.shape[0]
    for i in range(per):
        for s in range(8):
            for half in range(2):
                grads[me * per + i, s, pl.ds(half * 4, 4), :] = own[i, pl.ds(s * 4, 4), :]
                grads[(1 - me) * per + i, s, pl.ds(half * 4, 4), :] = other[i, pl.ds(s * 4, 4), :]
    for j in range(2):
        for s in range(8):
            search[s, pl.ds(j * 4, 4), :] = own[per + j, pl.ds(s * 4, 4), :]
    fisher_rows(prior, grads, search, weights_of(grads, search[...]), image)
    for s in range(8):
        payload[s] = image[...]


def advance(first, images, solution, residue, search, new_solution, new_residue, new_search):
    old = search[...]
    rest = old if first else residue[...]
    image = images[...]
    norm = inner(rest, rest)
    alpha = norm / inner(old, image)
    new_solution[...] = alpha * old if first else solution[...] + alpha * old
    rest = rest - alpha * image
    new_residue[...] = rest
    norm_next = inner(rest, rest)
    new_search[...] = rest + (norm_next / norm) * old
    return norm_next


def step_kernel(
    images, solution, residue, search, grads, prior,
    new_solution, new_residue, new_search, payload, image,
):
    advance(False, images, solution, residue, search, new_solution, new_residue, new_search)
    fisher_rows(prior, grads, new_search, weights_of(grads, new_search[...]), image)
    for s in range(8):
        payload[s] = image[...]


def first_kernel(
    images, search, grads, prior, new_solution, new_residue, new_search, payload, image
):
    advance(True, images, None, None, search, new_solution, new_residue, new_search)
    fisher_rows(prior, grads, new_search, weights_of(grads, new_search[...]), image)
    for s in range(8):
        payload[s] = image[...]


def last_kernel(
    images, solution, residue, search, grads, prior,
    own, payload, values, new_solution, new_residue, new_search, image,
):
    me = lax.axis_index("tensor")
    norm = advance(False, images, solution, residue, search, new_solution, new_residue, new_search)
    weights = weights_of(grads, new_search[...])
    fisher_rows(prior, grads, new_search, weights, image)
    curve = pair_sums(new_search[me] * image[...])
    for s in range(8):
        payload[s] = jnp.broadcast_to(curve, (8, LANES))
    own[0] = new_solution[me]
    own[1] = new_search[me]
    own[2] = jnp.broadcast_to(norm, (8, LANES))
    values[0] = jnp.broadcast_to(weights_of(grads, new_solution[...]), values.shape[1:])
    values[1] = jnp.broadcast_to(weights, values.shape[1:])


def end_kernel(curves, own, values, scores, solution):
    alpha = own[2] / jnp.sum(curves[...], axis=0)
    done = own[0] + alpha * own[1]
    for j in range(2):
        for c in range(4):
            solution[pl.ds(j, 1), pl.ds(c * LANES, LANES)] = done[j * 4 + c : j * 4 + c + 1]
    total = values.shape[1]
    lane = lax.broadcasted_iota(jnp.int32, (8, LANES), 1)
    table = jnp.zeros((8, LANES), jnp.float32)
    for i in range(total):
        table = jnp.where(lane == i, (values[0, i] + alpha * values[1, i]) / RANK, table)
    for j in range(2):
        scores[pl.ds(j, 1), :] = table[j * 4 : j * 4 + 1, :total]


def call(kernel, shapes, operands, scratch=(), limit=24):
    return pl.pallas_call(
        kernel,
        out_shape=[jax.ShapeDtypeStruct(s, jnp.float32) for s in shapes],
        in_specs=[VMEM] * len(operands),
        out_specs=[VMEM] * len(shapes),
        scratch_shapes=[pltpu.VMEM(s, jnp.float32) for s in scratch],
        compiler_params=pltpu.CompilerParams(vmem_limit_bytes=limit * 2**20),
        name=kernel.__name__,
    )(*operands)


def flipped(n, bit):
    return [(i, i ^ bit) for i in range(n)]


def per_device(
    train_inputs,
    train_outgrads,
    test_inputs,
    test_outgrads,
    train_counts,
    test_counts,
    proj_in,
    proj_out,
    fisher_prior,
):
    n = 8
    length = train_inputs.shape[1]
    counts = (train_counts, test_counts)
    operands = counts + (
        train_inputs, train_outgrads, test_inputs, test_outgrads, proj_in, proj_out
    )
    near = lambda x: lax.ppermute(x, "tensor", flipped(n, 1))
    next_to = lambda x: lax.ppermute(x, "tensor", flipped(n, 2))
    beyond = lambda x: lax.ppermute(x, "tensor", flipped(n, 4))
    (sent0,) = project_rows([(True, 0, 128, 128)], operands)
    got0 = near(sent0)
    (sent1,) = project_rows([(True, 128, 256, 256)], operands, (sent0,))
    got1 = near(sent1)
    (sent2,) = project_rows([(True, 384, 256, 256)], operands, (sent1,))
    got2 = near(sent2)
    kept01, sent3 = project_rows(
        [(False, 0, 384, 384), (True, 640, 256, 256)], operands, (sent2, got0)
    )
    got3 = near(sent3)
    theirs_a, ours_a = halve(0, 1, kept01, (got0, got1))
    half_a = next_to(theirs_a)
    kept2, sent4 = project_rows(
        [(False, 384, 256, 256), (True, 896, 128, 128)], operands, (sent3, theirs_a)
    )
    got4 = near(sent4)
    theirs_b, ours_b = halve(0, 1, kept2, (got2,))
    half_b = next_to(theirs_b)
    send_a, last_a = halve(0, 2, ours_a, (half_a,), (theirs_b,))
    whole_a = beyond(send_a)
    (kept34,) = project_rows([(False, 640, 384, 128)], operands, (sent4, theirs_b))
    theirs_c, ours_c = halve(0, 1, kept34, (got3,), (send_a,))
    half_c = next_to(theirs_c)
    send_b, last_b = halve(0, 2, ours_b, (half_b,), (theirs_c,))
    whole_b = beyond(send_b)
    theirs_d, ours_d = halve(256, 1, kept34, (got4,), (send_b,))
    half_d = next_to(theirs_d)
    send_c, last_c = halve(0, 2, ours_c, (half_c,), (theirs_d,))
    whole_c = beyond(send_c)
    send_d, last_d = halve(0, 2, ours_d, (half_d,), (send_c,))
    whole_d = beyond(send_d)
    square, prior = gram(
        0, length, counts, (last_a, last_b), (whole_a, whole_b), prior=fisher_prior
    )
    grad = gram(640, length, counts, (last_c, last_d), (whole_c, whole_d), before=square)
    own = lax.all_to_all(grad, "tensor", 0, 0, tiled=True)
    per = train_inputs.shape[0]
    other = lax.ppermute(own[:per], "dp", flipped(2, 1))
    state = (8, 8, LANES)
    piece = (8, LANES)
    total = 2 * per
    grads, search, payload = call(
        begin_kernel, [(total, 8, 8, LANES), state, state], (own, other, prior), [piece]
    )
    swap = lambda x: lax.all_to_all(x, "tensor", 0, 0, tiled=True)
    solution, residue, search, payload = call(
        first_kernel, [state] * 4, (swap(payload), search, grads, prior), [piece]
    )
    for _ in range(ITERS - 3):
        solution, residue, search, payload = call(
            step_kernel,
            [state] * 4,
            (swap(payload), solution, residue, search, grads, prior),
            [piece],
        )
    ours, payload, values = call(
        last_kernel,
        [(3, 8, LANES), state, (2, total, 8, LANES)],
        (swap(payload), solution, residue, search, grads, prior),
        [state, state, state, piece],
    )
    return tuple(
        call(
            end_kernel,
            [(2, total), (2, fisher_prior.shape[0])],
            (swap(payload), ours, values),
        )
    )


def solution(mesh):
    in_specs = (
        P(("parts", "dp"), None, "tensor"),
        P(("parts", "dp"), None, "tensor"),
        P(("parts", "dp"), None, "tensor"),
        P(("parts", "dp"), None, "tensor"),
        P(("parts", "dp")),
        P(("parts", "dp")),
        P(None, "tensor"),
        P(None, "tensor"),
        P(("parts", "tensor"), None),
    )
    out_specs = (P(("parts", "dp"), None), P(("parts", "dp"), "tensor"))
    body = per_device if mesh.shape["tensor"] == 8 and mesh.shape["dp"] == 2 else plain
    return jax.shard_map(
        body, mesh=mesh, in_specs=in_specs, out_specs=out_specs, check_vma=False
    )
```

```python
import functools
import math

import jax
import jax.numpy as jnp
from jax import lax
from jax.experimental import pallas as pl
from jax.experimental.pallas import tpu as pltpu
from jax.sharding import PartitionSpec as P

RANK = 64
ITERS = 6
LANES = 128
FLOOR = 256
SLOTS = 4
SMALL = 24 * 2**20

HIGH = lax.Precision.HIGHEST
VMEM = pl.BlockSpec(memory_space=pltpu.VMEM)
SMEM = pl.BlockSpec(memory_space=pltpu.SMEM)
ANY = pl.BlockSpec(memory_space=pl.ANY)


def project(data, basis):
    rows = data.reshape(-1, data.shape[-1])
    return lax.dot_general(
        rows, basis, (((1,), (1,)), ((), ())), preferred_element_type=jnp.float32
    )


def outer_sums(left, right, counts, length):
    examples = counts.shape[0]
    left = left.reshape(examples, length, -1)
    right = right.reshape(examples, length, -1)
    live = (jnp.arange(length, dtype=jnp.int32)[None, :] < counts[:, None]).astype(jnp.float32)
    grads = jnp.einsum("etr,ets->ers", left * live[:, :, None], right, precision=HIGH)
    return grads.reshape(examples, -1) * (1.0 / math.sqrt(length))


def plain(
    train_inputs,
    train_outgrads,
    test_inputs,
    test_outgrads,
    train_counts,
    test_counts,
    proj_in,
    proj_out,
    fisher_prior,
):
    length = train_inputs.shape[1]
    left_train = project(train_outgrads, proj_out)
    right_train = project(train_inputs, proj_in)
    left_test = project(test_outgrads, proj_out)
    right_test = project(test_inputs, proj_in)
    left_train, right_train, left_test, right_test = lax.psum(
        (left_train, right_train, left_test, right_test), "tensor"
    )
    train_grads = outer_sums(left_train, right_train, train_counts, length)
    test_grads = outer_sums(left_test, right_test, test_counts, length)
    every_train = lax.all_gather(train_grads, "dp", axis=0, tiled=True)
    total_train = every_train.shape[0]
    own_rows = fisher_prior.shape[0]
    start = lax.axis_index("tensor") * own_rows
    own_train = lax.dynamic_slice_in_dim(every_train, start, own_rows, 1)
    fisher_rows = fisher_prior + jnp.dot(own_train.T, every_train, precision=HIGH) / total_train
    residue = test_grads
    search = test_grads
    solution = jnp.zeros_like(test_grads)
    norm_now = jnp.sum(test_grads * test_grads, axis=1)
    for step in range(ITERS):
        part = lax.dot_general(search, fisher_rows, (((1,), (1,)), ((), ())), precision=HIGH)
        image = lax.all_gather(part, "tensor", axis=1, tiled=True)
        alpha = norm_now / jnp.sum(search * image, axis=1)
        solution = solution + alpha[:, None] * search
        residue = residue - alpha[:, None] * image
        norm_next = jnp.sum(residue * residue, axis=1)
        search = residue + (norm_next / norm_now)[:, None] * search
        norm_now = norm_next
    scores = jnp.dot(solution, every_train.T, precision=HIGH) / RANK
    return (scores, lax.dynamic_slice_in_dim(solution, start, own_rows, 1))


def project_kernel(
    parts, tile, after, train_count, test_count, train_in, train_out, test_in, test_out,
    basis_in, basis_out, *rest,
):
    outs = rest[after : after + sum(len(part[2]) for part in parts)]
    held_in, held_out, near_in, near_out, of_train, of_test, sems, more = rest[after + len(outs) :]
    me = lax.rem(lax.axis_index("tensor"), 2)
    last = train_in.shape[0] // 2
    total = 4 * len(parts)
    dynamic = any(first >= FLOOR for _, first, _ in parts)

    def pick(part, values):
        value = jnp.int32(values[0])
        for g in range(1, len(values)):
            value = jnp.where(part == g, values[g], value)
        return value

    def place(k):
        part = k // 4
        low = pick(part, [int(p[0]) for p in parts]) ^ me
        return lax.rem(k, 4), pl.multiple_of(pick(part, [p[1] for p in parts]), LANES), low

    def live(k):
        if not dynamic:
            return jnp.bool_(True)
        i, row, low = place(k)
        train = of_train[jnp.minimum(2 * i + low, 2 * last - 1)]
        return (jnp.where(i < last, train, of_test[low]) > row) | (k == 0)

    def copies(k, train):
        i, row, low = place(k)
        slot = lax.rem(k, SLOTS)
        rows = pl.ds(row, tile)
        wide, narrow, e = (train_in, train_out, 2 * i + low) if train else (test_in, test_out, low)
        return (
            pltpu.make_async_copy(wide.at[e, rows], held_in.at[slot], sems.at[slot, 0]),
            pltpu.make_async_copy(narrow.at[e, rows], held_out.at[slot], sems.at[slot, 1]),
        )

    def start(k):
        mine = (k < total) & live(k)
        i = lax.rem(k, 4)

        @pl.when(mine & (i < last))
        def _():
            for copy in copies(k, True):
                copy.start()

        @pl.when(mine & (i == last))
        def _():
            for copy in copies(k, False):
                copy.start()

    bases = (
        pltpu.make_async_copy(basis_in, near_in, more.at[0]),
        pltpu.make_async_copy(basis_out, near_out, more.at[1]),
    )
    if dynamic:
        lengths = (
            pltpu.make_async_copy(train_count, of_train, more.at[2]),
            pltpu.make_async_copy(test_count, of_test, more.at[3]),
        )
        for copy in lengths:
            copy.start()
    for copy in copies(jnp.int32(0), True) + bases:
        copy.start()
    if dynamic:
        for copy in lengths:
            copy.wait()

    @pl.loop(1, SLOTS - 1)
    def _(k):
        start(k)

    for copy in bases:
        copy.wait()

    @pl.loop(0, total)
    def _(k):
        i, _, _ = place(k)
        slot = lax.rem(k, SLOTS)
        start(k + SLOTS - 1)

        def keep(rows):
            at = 0
            for g, (_, _, pieces) in enumerate(parts):

                @pl.when(k // 4 == g)
                def _():
                    done = 0
                    for n, size in enumerate(pieces):
                        outs[at + n][i] = rows[done : done + size]
                        done += size

                at += len(pieces)

        def make():
            for copy in copies(k, False):
                copy.wait()
            dims = (((1,), (1,)), ((), ()))
            left = lax.dot_general(
                held_out[slot], near_out[...], dims, preferred_element_type=jnp.float32
            )
            right = lax.dot_general(
                held_in[slot], near_in[...], dims, preferred_element_type=jnp.float32
            )
            keep(jnp.concatenate([left, right], axis=1))

        if dynamic:
            alive = live(k)
            pl.when(alive)(make)

            @pl.when(jnp.logical_not(alive))
            def _():
                keep(jnp.zeros((tile, LANES), jnp.float32))

        else:
            make()


def in_hbm(arrays):
    return [pltpu.with_memory_space_constraint(x, pltpu.HBM) for x in arrays]


def project_rows(parts, operands, after=()):
    wide, narrow, basis_in, basis_out = operands[2], operands[3], operands[6], operands[7]
    tile = sum(parts[0][2])
    sizes = [size for part in parts for size in part[2]]
    rows = 4 * sum(sizes)
    depth = wide.shape[2] + narrow.shape[2]
    return pl.pallas_call(
        functools.partial(project_kernel, parts, tile, len(after)),
        out_shape=[pltpu.VMEM((4, size, LANES), jnp.float32) for size in sizes],
        in_specs=[ANY] * (len(operands) + len(after)),
        out_specs=[VMEM] * len(sizes),
        scratch_shapes=[
            pltpu.VMEM((SLOTS, tile, wide.shape[2]), wide.dtype),
            pltpu.VMEM((SLOTS, tile, narrow.shape[2]), narrow.dtype),
            pltpu.VMEM(basis_in.shape, basis_in.dtype),
            pltpu.VMEM(basis_out.shape, basis_out.dtype),
            pltpu.SMEM(operands[0].shape, jnp.int32),
            pltpu.SMEM(operands[1].shape, jnp.int32),
            pltpu.SemaphoreType.DMA((SLOTS, 2)),
            pltpu.SemaphoreType.DMA((4,)),
        ],
        compiler_params=pltpu.CompilerParams(vmem_limit_bytes=SMALL),
        cost_estimate=pl.CostEstimate(
            flops=2 * rows * depth * RANK, bytes_accessed=rows * depth * 2, transcendentals=0
        ),
        name="project_" + "_".join(f"{'send' if p[0] else 'keep'}{p[1]}" for p in parts),
    )(*in_hbm(operands), *after)


def halve_kernel(offset, bit, pieces, kept, *rest):
    got, (theirs, ours) = rest[:pieces], rest[-2:]
    mine = (lax.axis_index("tensor") >> bit) & 1
    groups = theirs.shape[0]
    at = 0
    for piece in got:
        rows = piece.shape[1]
        here, there = pl.ds(offset + at, rows), pl.ds(at, rows)
        for h in range(groups):
            give = 2 * h + 1 - mine if bit == 1 else 1 - mine
            take = 2 * h + mine if bit == 1 else mine
            theirs[h, there, :] = kept[give, here, :] + piece[give, :, :]
            ours[h, there, :] = kept[take, here, :] + piece[take, :, :]
        at += rows


def halve(offset, bit, kept, got, after=()):
    rows = sum(piece.shape[1] for piece in got)
    shape = pltpu.VMEM((kept.shape[0] // 2, rows, LANES), jnp.float32)
    return pl.pallas_call(
        functools.partial(halve_kernel, offset, bit, len(got)),
        out_shape=[shape, shape],
        in_specs=[VMEM] * (1 + len(got)) + [ANY] * len(after),
        out_specs=[VMEM, VMEM],
        compiler_params=pltpu.CompilerParams(vmem_limit_bytes=SMALL),
        name=f"halve{bit}",
    )(kept, *got, *after)


def gram_kernel(first, pieces, length, final, train_count, test_count, *rest):
    ours, got = rest[:pieces], rest[pieces : 2 * pieces]
    rest = rest[2 * pieces :]
    if final:
        before, out, held, of_train, of_test, sems = rest
    else:
        prior, out, near, of_train, of_test, sems, more = rest
        fetch = pltpu.make_async_copy(prior, near, more)
        fetch.start()
    me = lax.axis_index("tensor")
    train = train_count.shape[0]
    lengths = (
        pltpu.make_async_copy(train_count, of_train, sems.at[0]),
        pltpu.make_async_copy(test_count, of_test, sems.at[1]),
    )
    for copy in lengths:
        copy.start()
    for copy in lengths:
        copy.wait()
    count = jnp.where(
        me < train, of_train[jnp.minimum(me, train - 1)], of_test[jnp.maximum(me - train, 0)]
    )
    total = before[...] if final else jnp.zeros((RANK, RANK), jnp.float32)
    for a, b in zip(ours, got):
        rows = a[0] + b[0]
        live = lax.broadcasted_iota(jnp.int32, rows.shape, 0) + first < count
        rows = jnp.where(live, rows, 0.0)
        total = total + lax.dot_general(
            rows[:, :RANK], rows[:, RANK:], (((0,), (0,)), ((), ())), precision=HIGH,
            preferred_element_type=jnp.float32,
        )
        first += rows.shape[0]
    if not final:
        out[...] = total
        fetch.wait()
        return
    held[...] = total * (1.0 / math.sqrt(length))
    half = RANK // 2
    grad = jnp.concatenate(
        [held[pl.ds(0, half, stride=2), :], held[pl.ds(1, half, stride=2), :]], axis=1
    )
    for i in range(out.shape[0]):
        out[i] = grad


def gram(first, length, counts, ours, got, prior=None, before=None):
    final = before is not None
    square = jax.ShapeDtypeStruct((RANK, RANK), jnp.float32)
    scratch = [pltpu.SMEM(c.shape, jnp.int32) for c in counts] + [pltpu.SemaphoreType.DMA((2,))]
    if final:
        out_shape = jax.ShapeDtypeStruct((8, RANK // 2, LANES), jnp.float32)
        scratch = [pltpu.VMEM((RANK, RANK), jnp.float32)] + scratch
    else:
        out_shape = [square, pltpu.VMEM(prior.shape, prior.dtype)]
        counts, (prior,) = in_hbm(counts), in_hbm([prior])
        scratch = scratch + [pltpu.SemaphoreType.DMA]
    return pl.pallas_call(
        functools.partial(gram_kernel, first, len(ours), length, final),
        out_shape=out_shape,
        in_specs=[ANY, ANY] + [VMEM] * (2 * len(ours)) + [VMEM if final else ANY],
        out_specs=VMEM if final else [VMEM, VMEM],
        scratch_shapes=scratch,
        compiler_params=pltpu.CompilerParams(vmem_limit_bytes=SMALL),
        name="gram_end" if final else "gram_begin",
    )(*counts, *ours, *got, before if final else prior)


def pair_sums(x):
    x = jnp.sum(x, axis=-1, keepdims=True)
    upper = lax.broadcasted_iota(jnp.int32, x.shape, x.ndim - 2) < 4
    first = jnp.sum(jnp.where(upper, x, 0.0), axis=-2, keepdims=True)
    second = jnp.sum(jnp.where(upper, 0.0, x), axis=-2, keepdims=True)
    return jnp.where(upper, first, second)


def inner(a, b):
    return pair_sums(jnp.sum(a * b, axis=0))


def weights_of(grads, vector):
    return pair_sums(
        jnp.stack([jnp.sum(grads[i] * vector, axis=0) for i in range(grads.shape[0])])
    )


def fisher_rows(prior, grads, vector, weights, image):
    me = lax.axis_index("tensor")

    @pl.loop(0, prior.shape[0] // LANES)
    def _(block):
        rows = pl.ds(pl.multiple_of(block * LANES, LANES), LANES)
        sums = [jnp.zeros((LANES, LANES), jnp.float32)] * 2
        for c in range(prior.shape[1] // LANES):
            piece = prior[rows, pl.ds(c * LANES, LANES)]
            for j in range(2):
                sums[j] = sums[j] + piece * vector[c // 4, pl.ds(j * 4 + c % 4, 1), :]
        for j in range(2):
            line = jnp.sum(sums[j].T, axis=0, keepdims=True)
            image[pl.ds(j * 4 + block, 1), :] = line

    total = grads.shape[0]
    low = weights[0] * grads[0, me]
    for i in range(1, total):
        low = low + weights[i] * grads[i, me]
    image[...] = image[...] + low * (1.0 / total)


def begin_kernel(own, other, prior, grads, search, payload, image):
    me = lax.axis_index("dp")
    per = other.shape[0]
    for i in range(per):
        for s in range(8):
            for half in range(2):
                grads[me * per + i, s, pl.ds(half * 4, 4), :] = own[i, pl.ds(s * 4, 4), :]
                grads[(1 - me) * per + i, s, pl.ds(half * 4, 4), :] = other[i, pl.ds(s * 4, 4), :]
    for j in range(2):
        for s in range(8):
            search[s, pl.ds(j * 4, 4), :] = own[per + j, pl.ds(s * 4, 4), :]
    fisher_rows(prior, grads, search, weights_of(grads, search[...]), image)
    for s in range(8):
        payload[s] = image[...]


def advance(first, images, solution, residue, search, new_solution, new_residue, new_search):
    old = search[...]
    rest = old if first else residue[...]
    image = images[...]
    norm = inner(rest, rest)
    alpha = norm / inner(old, image)
    new_solution[...] = alpha * old if first else solution[...] + alpha * old
    rest = rest - alpha * image
    new_residue[...] = rest
    norm_next = inner(rest, rest)
    new_search[...] = rest + (norm_next / norm) * old
    return norm_next


def step_kernel(
    images, solution, residue, search, grads, prior,
    new_solution, new_residue, new_search, payload, image,
):
    advance(False, images, solution, residue, search, new_solution, new_residue, new_search)
    fisher_rows(prior, grads, new_search, weights_of(grads, new_search[...]), image)
    for s in range(8):
        payload[s] = image[...]


def first_kernel(
    images, search, grads, prior, new_solution, new_residue, new_search, payload, image
):
    advance(True, images, None, None, search, new_solution, new_residue, new_search)
    fisher_rows(prior, grads, new_search, weights_of(grads, new_search[...]), image)
    for s in range(8):
        payload[s] = image[...]


def last_kernel(
    images, solution, residue, search, grads, prior,
    own, payload, values, new_solution, new_residue, new_search, image,
):
    me = lax.axis_index("tensor")
    norm = advance(False, images, solution, residue, search, new_solution, new_residue, new_search)
    weights = weights_of(grads, new_search[...])
    fisher_rows(prior, grads, new_search, weights, image)
    curve = pair_sums(new_search[me] * image[...])
    for s in range(8):
        payload[s] = jnp.broadcast_to(curve, (8, LANES))
    own[0] = new_solution[me]
    own[1] = new_search[me]
    own[2] = jnp.broadcast_to(norm, (8, LANES))
    values[0] = jnp.broadcast_to(weights_of(grads, new_solution[...]), values.shape[1:])
    values[1] = jnp.broadcast_to(weights, values.shape[1:])


def end_kernel(curves, own, values, scores, solution):
    alpha = own[2] / jnp.sum(curves[...], axis=0)
    done = own[0] + alpha * own[1]
    for j in range(2):
        for c in range(4):
            solution[pl.ds(j, 1), pl.ds(c * LANES, LANES)] = done[j * 4 + c : j * 4 + c + 1]
    total = values.shape[1]
    lane = lax.broadcasted_iota(jnp.int32, (8, LANES), 1)
    table = jnp.zeros((8, LANES), jnp.float32)
    for i in range(total):
        table = jnp.where(lane == i, (values[0, i] + alpha * values[1, i]) / RANK, table)
    for j in range(2):
        scores[pl.ds(j, 1), :] = table[j * 4 : j * 4 + 1, :total]


def call(kernel, shapes, operands, scratch=(), limit=24):
    return pl.pallas_call(
        kernel,
        out_shape=[jax.ShapeDtypeStruct(s, jnp.float32) for s in shapes],
        in_specs=[VMEM] * len(operands),
        out_specs=[VMEM] * len(shapes),
        scratch_shapes=[pltpu.VMEM(s, jnp.float32) for s in scratch],
        compiler_params=pltpu.CompilerParams(vmem_limit_bytes=limit * 2**20),
        name=kernel.__name__,
    )(*operands)


def flipped(n, bit):
    return [(i, i ^ bit) for i in range(n)]


def per_device(
    train_inputs,
    train_outgrads,
    test_inputs,
    test_outgrads,
    train_counts,
    test_counts,
    proj_in,
    proj_out,
    fisher_prior,
):
    n = 8
    length = train_inputs.shape[1]
    counts = (train_counts, test_counts)
    operands = counts + (
        train_inputs, train_outgrads, test_inputs, test_outgrads, proj_in, proj_out
    )
    near = lambda x: lax.ppermute(x, "tensor", flipped(n, 1))
    next_to = lambda x: lax.ppermute(x, "tensor", flipped(n, 2))
    beyond = lambda x: lax.ppermute(x, "tensor", flipped(n, 4))
    (sent0,) = project_rows([(True, 0, (256,))], operands)
    got0 = near(sent0)
    (sent1,) = project_rows([(True, 256, (256,))], operands, (sent0,))
    got1 = near(sent1)
    kept0, sent2 = project_rows([(False, 0, (256,)), (True, 512, (256,))], operands, (sent1,))
    got2 = near(sent2)
    theirs_a, ours_a = halve(0, 1, kept0, (got0,))
    half_a = next_to(theirs_a)
    kept1, sent3, sent4 = project_rows(
        [(False, 256, (256,)), (True, 768, (128, 128))], operands, (sent2, theirs_a)
    )
    got3 = near(sent3)
    got4 = near(sent4)
    theirs_b, ours_b = halve(0, 1, kept1, (got1,))
    half_b = next_to(theirs_b)
    send_a, last_a = halve(0, 2, ours_a, (half_a,), (theirs_b,))
    whole_a = beyond(send_a)
    kept2, kept3 = project_rows(
        [(False, 512, (256,)), (False, 768, (256,))], operands, (sent4, send_a)
    )
    theirs_c, ours_c = halve(0, 1, kept2, (got2,), (whole_a,))
    half_c = next_to(theirs_c)
    send_b, last_b = halve(0, 2, ours_b, (half_b,), (theirs_c,))
    whole_b = beyond(send_b)
    theirs_d, ours_d = halve(0, 1, kept3, (got3,), (send_b,))
    half_d = next_to(theirs_d)
    theirs_e, ours_e = halve(128, 1, kept3, (got4,), (theirs_d,))
    half_e = next_to(theirs_e)
    send_c, last_c = halve(0, 2, ours_c, (half_c,), (theirs_e, whole_b))
    whole_c = beyond(send_c)
    send_d, last_d = halve(0, 2, ours_d, (half_d,), (send_c,))
    whole_d = beyond(send_d)
    send_e, last_e = halve(0, 2, ours_e, (half_e,), (send_d,))
    whole_e = beyond(send_e)
    square, prior = gram(
        0, length, counts, (last_a, last_b, last_c), (whole_a, whole_b, whole_c), prior=fisher_prior
    )
    grad = gram(768, length, counts, (last_d, last_e), (whole_d, whole_e), before=square)
    own = lax.all_to_all(grad, "tensor", 0, 0, tiled=True)
    per = train_inputs.shape[0]
    other = lax.ppermute(own[:per], "dp", flipped(2, 1))
    state = (8, 8, LANES)
    piece = (8, LANES)
    total = 2 * per
    grads, search, payload = call(
        begin_kernel, [(total, 8, 8, LANES), state, state], (own, other, prior), [piece]
    )
    swap = lambda x: lax.all_to_all(x, "tensor", 0, 0, tiled=True)
    solution, residue, search, payload = call(
        first_kernel, [state] * 4, (swap(payload), search, grads, prior), [piece]
    )
    for _ in range(ITERS - 3):
        solution, residue, search, payload = call(
            step_kernel,
            [state] * 4,
            (swap(payload), solution, residue, search, grads, prior),
            [piece],
        )
    ours, payload, values = call(
        last_kernel,
        [(3, 8, LANES), state, (2, total, 8, LANES)],
        (swap(payload), solution, residue, search, grads, prior),
        [state, state, state, piece],
    )
    return tuple(
        call(
            end_kernel,
            [(2, total), (2, fisher_prior.shape[0])],
            (swap(payload), ours, values),
        )
    )


def solution(mesh):
    in_specs = (
        P(("parts", "dp"), None, "tensor"),
        P(("parts", "dp"), None, "tensor"),
        P(("parts", "dp"), None, "tensor"),
        P(("parts", "dp"), None, "tensor"),
        P(("parts", "dp")),
        P(("parts", "dp")),
        P(None, "tensor"),
        P(None, "tensor"),
        P(("parts", "tensor"), None),
    )
    out_specs = (P(("parts", "dp"), None), P(("parts", "dp"), "tensor"))
    body = per_device if mesh.shape["tensor"] == 8 and mesh.shape["dp"] == 2 else plain
    return jax.shard_map(
        body, mesh=mesh, in_specs=in_specs, out_specs=out_specs, check_vma=False
    )
```

```python
import functools
import math

import jax
import jax.numpy as jnp
from jax import lax
from jax.experimental import pallas as pl
from jax.experimental.pallas import tpu as pltpu
from jax.sharding import PartitionSpec as P

RANK = 64
ITERS = 6
LANES = 128
FLOOR = 256
SLOTS = 4
SMALL = 24 * 2**20

HIGH = lax.Precision.HIGHEST
VMEM = pl.BlockSpec(memory_space=pltpu.VMEM)
SMEM = pl.BlockSpec(memory_space=pltpu.SMEM)
ANY = pl.BlockSpec(memory_space=pl.ANY)


def project(data, basis):
    rows = data.reshape(-1, data.shape[-1])
    return lax.dot_general(
        rows, basis, (((1,), (1,)), ((), ())), preferred_element_type=jnp.float32
    )


def outer_sums(left, right, counts, length):
    examples = counts.shape[0]
    left = left.reshape(examples, length, -1)
    right = right.reshape(examples, length, -1)
    live = (jnp.arange(length, dtype=jnp.int32)[None, :] < counts[:, None]).astype(jnp.float32)
    grads = jnp.einsum("etr,ets->ers", left * live[:, :, None], right, precision=HIGH)
    return grads.reshape(examples, -1) * (1.0 / math.sqrt(length))


def plain(
    train_inputs,
    train_outgrads,
    test_inputs,
    test_outgrads,
    train_counts,
    test_counts,
    proj_in,
    proj_out,
    fisher_prior,
):
    length = train_inputs.shape[1]
    left_train = project(train_outgrads, proj_out)
    right_train = project(train_inputs, proj_in)
    left_test = project(test_outgrads, proj_out)
    right_test = project(test_inputs, proj_in)
    left_train, right_train, left_test, right_test = lax.psum(
        (left_train, right_train, left_test, right_test), "tensor"
    )
    train_grads = outer_sums(left_train, right_train, train_counts, length)
    test_grads = outer_sums(left_test, right_test, test_counts, length)
    every_train = lax.all_gather(train_grads, "dp", axis=0, tiled=True)
    total_train = every_train.shape[0]
    own_rows = fisher_prior.shape[0]
    start = lax.axis_index("tensor") * own_rows
    own_train = lax.dynamic_slice_in_dim(every_train, start, own_rows, 1)
    fisher_rows = fisher_prior + jnp.dot(own_train.T, every_train, precision=HIGH) / total_train
    residue = test_grads
    search = test_grads
    solution = jnp.zeros_like(test_grads)
    norm_now = jnp.sum(test_grads * test_grads, axis=1)
    for step in range(ITERS):
        part = lax.dot_general(search, fisher_rows, (((1,), (1,)), ((), ())), precision=HIGH)
        image = lax.all_gather(part, "tensor", axis=1, tiled=True)
        alpha = norm_now / jnp.sum(search * image, axis=1)
        solution = solution + alpha[:, None] * search
        residue = residue - alpha[:, None] * image
        norm_next = jnp.sum(residue * residue, axis=1)
        search = residue + (norm_next / norm_now)[:, None] * search
        norm_now = norm_next
    scores = jnp.dot(solution, every_train.T, precision=HIGH) / RANK
    return (scores, lax.dynamic_slice_in_dim(solution, start, own_rows, 1))


def project_kernel(
    parts, tile, after, train_count, test_count, train_in, train_out, test_in, test_out,
    basis_in, basis_out, *rest,
):
    outs = rest[after : after + sum(len(part[2]) for part in parts)]
    held_in, held_out, near_in, near_out, of_train, of_test, sems, more = rest[after + len(outs) :]
    me = lax.rem(lax.axis_index("tensor"), 2)
    last = train_in.shape[0] // 2
    total = 4 * len(parts)
    dynamic = any(first >= FLOOR for _, first, _ in parts)

    def pick(part, values):
        value = jnp.int32(values[0])
        for g in range(1, len(values)):
            value = jnp.where(part == g, values[g], value)
        return value

    def place(k):
        part = k // 4
        low = pick(part, [int(p[0]) for p in parts]) ^ me
        return lax.rem(k, 4), pl.multiple_of(pick(part, [p[1] for p in parts]), LANES), low

    def live(k):
        if not dynamic:
            return jnp.bool_(True)
        i, row, low = place(k)
        train = of_train[jnp.minimum(2 * i + low, 2 * last - 1)]
        return (jnp.where(i < last, train, of_test[low]) > row) | (k == 0)

    def copies(k, train):
        i, row, low = place(k)
        slot = lax.rem(k, SLOTS)
        rows = pl.ds(row, tile)
        wide, narrow, e = (train_in, train_out, 2 * i + low) if train else (test_in, test_out, low)
        return (
            pltpu.make_async_copy(wide.at[e, rows], held_in.at[slot], sems.at[slot, 0]),
            pltpu.make_async_copy(narrow.at[e, rows], held_out.at[slot], sems.at[slot, 1]),
        )

    def start(k):
        mine = (k < total) & live(k)
        i = lax.rem(k, 4)

        @pl.when(mine & (i < last))
        def _():
            for copy in copies(k, True):
                copy.start()

        @pl.when(mine & (i == last))
        def _():
            for copy in copies(k, False):
                copy.start()

    bases = (
        pltpu.make_async_copy(basis_in, near_in, more.at[0]),
        pltpu.make_async_copy(basis_out, near_out, more.at[1]),
    )
    if dynamic:
        lengths = (
            pltpu.make_async_copy(train_count, of_train, more.at[2]),
            pltpu.make_async_copy(test_count, of_test, more.at[3]),
        )
        for copy in lengths:
            copy.start()
    for copy in copies(jnp.int32(0), True) + bases:
        copy.start()
    if dynamic:
        for copy in lengths:
            copy.wait()

    @pl.loop(1, SLOTS - 1)
    def _(k):
        start(k)

    for copy in bases:
        copy.wait()

    @pl.loop(0, total)
    def _(k):
        i, _, _ = place(k)
        slot = lax.rem(k, SLOTS)
        start(k + SLOTS - 1)

        def keep(rows):
            at = 0
            for g, (_, _, pieces) in enumerate(parts):

                @pl.when(k // 4 == g)
                def _():
                    done = 0
                    for n, size in enumerate(pieces):
                        outs[at + n][i] = rows[done : done + size]
                        done += size

                at += len(pieces)

        def make():
            for copy in copies(k, False):
                copy.wait()
            dims = (((1,), (1,)), ((), ()))
            left = lax.dot_general(
                held_out[slot], near_out[...], dims, preferred_element_type=jnp.float32
            )
            right = lax.dot_general(
                held_in[slot], near_in[...], dims, preferred_element_type=jnp.float32
            )
            keep(jnp.concatenate([left, right], axis=1))

        if dynamic:
            alive = live(k)
            pl.when(alive)(make)

            @pl.when(jnp.logical_not(alive))
            def _():
                keep(jnp.zeros((tile, LANES), jnp.float32))

        else:
            make()


def in_hbm(arrays):
    return [pltpu.with_memory_space_constraint(x, pltpu.HBM) for x in arrays]


def project_rows(parts, operands, after=()):
    wide, narrow, basis_in, basis_out = operands[2], operands[3], operands[6], operands[7]
    tile = sum(parts[0][2])
    sizes = [size for part in parts for size in part[2]]
    rows = 4 * sum(sizes)
    depth = wide.shape[2] + narrow.shape[2]
    return pl.pallas_call(
        functools.partial(project_kernel, parts, tile, len(after)),
        out_shape=[pltpu.VMEM((4, size, LANES), jnp.float32) for size in sizes],
        in_specs=[ANY] * (len(operands) + len(after)),
        out_specs=[VMEM] * len(sizes),
        scratch_shapes=[
            pltpu.VMEM((SLOTS, tile, wide.shape[2]), wide.dtype),
            pltpu.VMEM((SLOTS, tile, narrow.shape[2]), narrow.dtype),
            pltpu.VMEM(basis_in.shape, basis_in.dtype),
            pltpu.VMEM(basis_out.shape, basis_out.dtype),
            pltpu.SMEM(operands[0].shape, jnp.int32),
            pltpu.SMEM(operands[1].shape, jnp.int32),
            pltpu.SemaphoreType.DMA((SLOTS, 2)),
            pltpu.SemaphoreType.DMA((4,)),
        ],
        compiler_params=pltpu.CompilerParams(vmem_limit_bytes=SMALL),
        cost_estimate=pl.CostEstimate(
            flops=2 * rows * depth * RANK, bytes_accessed=rows * depth * 2, transcendentals=0
        ),
        name="project_" + "_".join(f"{'send' if p[0] else 'keep'}{p[1]}" for p in parts),
    )(*in_hbm(operands), *after)


def halve_kernel(offsets, bit, *refs):
    pairs = len(offsets)
    kept, got, (theirs, ours) = refs[:pairs], refs[pairs : 2 * pairs], refs[-2:]
    mine = (lax.axis_index("tensor") >> bit) & 1
    at = 0
    for offset, base, piece in zip(offsets, kept, got):
        rows = piece.shape[1]
        here, there = pl.ds(offset, rows), pl.ds(at, rows)
        for h in range(theirs.shape[0]):
            give = 2 * h + 1 - mine if bit == 1 else 1 - mine
            take = 2 * h + mine if bit == 1 else mine
            theirs[h, there, :] = base[give, here, :] + piece[give, :, :]
            ours[h, there, :] = base[take, here, :] + piece[take, :, :]
        at += rows


def halve(bit, pairs, after=()):
    kept, offsets, got = zip(*pairs)
    rows = sum(piece.shape[1] for piece in got)
    shape = pltpu.VMEM((kept[0].shape[0] // 2, rows, LANES), jnp.float32)
    return pl.pallas_call(
        functools.partial(halve_kernel, offsets, bit),
        out_shape=[shape, shape],
        in_specs=[VMEM] * (2 * len(pairs)) + [ANY] * len(after),
        out_specs=[VMEM, VMEM],
        compiler_params=pltpu.CompilerParams(vmem_limit_bytes=SMALL),
        name=f"halve{bit}",
    )(*kept, *got, *after)


def gram_kernel(first, pieces, length, final, train_count, test_count, *rest):
    ours, got = rest[:pieces], rest[pieces : 2 * pieces]
    rest = rest[2 * pieces :]
    if final:
        before, out, held, of_train, of_test, sems = rest
    else:
        prior, out, near, of_train, of_test, sems, more = rest
        fetch = pltpu.make_async_copy(prior, near, more)
        fetch.start()
    me = lax.axis_index("tensor")
    train = train_count.shape[0]
    lengths = (
        pltpu.make_async_copy(train_count, of_train, sems.at[0]),
        pltpu.make_async_copy(test_count, of_test, sems.at[1]),
    )
    for copy in lengths:
        copy.start()
    for copy in lengths:
        copy.wait()
    count = jnp.where(
        me < train, of_train[jnp.minimum(me, train - 1)], of_test[jnp.maximum(me - train, 0)]
    )
    total = before[...] if final else jnp.zeros((RANK, RANK), jnp.float32)
    for a, b in zip(ours, got):
        rows = a[0] + b[0]
        live = lax.broadcasted_iota(jnp.int32, rows.shape, 0) + first < count
        rows = jnp.where(live, rows, 0.0)
        total = total + lax.dot_general(
            rows[:, :RANK], rows[:, RANK:], (((0,), (0,)), ((), ())), precision=HIGH,
            preferred_element_type=jnp.float32,
        )
        first += rows.shape[0]
    if not final:
        out[...] = total
        fetch.wait()
        return
    held[...] = total * (1.0 / math.sqrt(length))
    half = RANK // 2
    grad = jnp.concatenate(
        [held[pl.ds(0, half, stride=2), :], held[pl.ds(1, half, stride=2), :]], axis=1
    )
    for i in range(out.shape[0]):
        out[i] = grad


def gram(first, length, counts, ours, got, prior=None, before=None):
    final = before is not None
    square = jax.ShapeDtypeStruct((RANK, RANK), jnp.float32)
    scratch = [pltpu.SMEM(c.shape, jnp.int32) for c in counts] + [pltpu.SemaphoreType.DMA((2,))]
    if final:
        out_shape = jax.ShapeDtypeStruct((8, RANK // 2, LANES), jnp.float32)
        scratch = [pltpu.VMEM((RANK, RANK), jnp.float32)] + scratch
    else:
        out_shape = [square, pltpu.VMEM(prior.shape, prior.dtype)]
        counts, (prior,) = in_hbm(counts), in_hbm([prior])
        scratch = scratch + [pltpu.SemaphoreType.DMA]
    return pl.pallas_call(
        functools.partial(gram_kernel, first, len(ours), length, final),
        out_shape=out_shape,
        in_specs=[ANY, ANY] + [VMEM] * (2 * len(ours)) + [VMEM if final else ANY],
        out_specs=VMEM if final else [VMEM, VMEM],
        scratch_shapes=scratch,
        compiler_params=pltpu.CompilerParams(vmem_limit_bytes=SMALL),
        name="gram_end" if final else "gram_begin",
    )(*counts, *ours, *got, before if final else prior)


def pair_sums(x):
    x = jnp.sum(x, axis=-1, keepdims=True)
    upper = lax.broadcasted_iota(jnp.int32, x.shape, x.ndim - 2) < 4
    first = jnp.sum(jnp.where(upper, x, 0.0), axis=-2, keepdims=True)
    second = jnp.sum(jnp.where(upper, 0.0, x), axis=-2, keepdims=True)
    return jnp.where(upper, first, second)


def inner(a, b):
    return pair_sums(jnp.sum(a * b, axis=0))


def weights_of(grads, vector):
    return pair_sums(
        jnp.stack([jnp.sum(grads[i] * vector, axis=0) for i in range(grads.shape[0])])
    )


def fisher_rows(prior, grads, vector, weights, image):
    me = lax.axis_index("tensor")

    @pl.loop(0, prior.shape[0] // LANES)
    def _(block):
        rows = pl.ds(pl.multiple_of(block * LANES, LANES), LANES)
        sums = [jnp.zeros((LANES, LANES), jnp.float32)] * 2
        for c in range(prior.shape[1] // LANES):
            piece = prior[rows, pl.ds(c * LANES, LANES)]
            for j in range(2):
                sums[j] = sums[j] + piece * vector[c // 4, pl.ds(j * 4 + c % 4, 1), :]
        for j in range(2):
            line = jnp.sum(sums[j].T, axis=0, keepdims=True)
            image[pl.ds(j * 4 + block, 1), :] = line

    total = grads.shape[0]
    low = weights[0] * grads[0, me]
    for i in range(1, total):
        low = low + weights[i] * grads[i, me]
    image[...] = image[...] + low * (1.0 / total)


def begin_kernel(own, other, prior, grads, search, payload, image):
    me = lax.axis_index("dp")
    per = grads.shape[0] // 2
    for i in range(per):
        at = ORDER.index(i)
        for s in range(8):
            for half in range(2):
                there, here = pl.ds(half * 4, 4), pl.ds(s * 4, 4)
                grads[me * per + i, s, there, :] = own[at, here, :]
                grads[(1 - me) * per + i, s, there, :] = other[at, here, :]
    for j in range(2):
        for s in range(8):
            search[s, pl.ds(j * 4, 4), :] = own[ORDER.index(per + j), pl.ds(s * 4, 4), :]
    fisher_rows(prior, grads, search, weights_of(grads, search[...]), image)
    for s in range(8):
        payload[s] = image[...]


def advance(first, images, solution, residue, search, new_solution, new_residue, new_search):
    old = search[...]
    rest = old if first else residue[...]
    image = jnp.stack([images[ORDER.index(s)] for s in range(8)])
    norm = inner(rest, rest)
    alpha = norm / inner(old, image)
    new_solution[...] = alpha * old if first else solution[...] + alpha * old
    rest = rest - alpha * image
    new_residue[...] = rest
    norm_next = inner(rest, rest)
    new_search[...] = rest + (norm_next / norm) * old
    return norm_next


def step_kernel(
    images, solution, residue, search, grads, prior,
    new_solution, new_residue, new_search, payload, image,
):
    advance(False, images, solution, residue, search, new_solution, new_residue, new_search)
    fisher_rows(prior, grads, new_search, weights_of(grads, new_search[...]), image)
    for s in range(8):
        payload[s] = image[...]


def first_kernel(
    images, search, grads, prior, new_solution, new_residue, new_search, payload, image
):
    advance(True, images, None, None, search, new_solution, new_residue, new_search)
    fisher_rows(prior, grads, new_search, weights_of(grads, new_search[...]), image)
    for s in range(8):
        payload[s] = image[...]


def last_kernel(
    images, solution, residue, search, grads, prior,
    own, payload, values, new_solution, new_residue, new_search, image,
):
    me = lax.axis_index("tensor")
    norm = advance(False, images, solution, residue, search, new_solution, new_residue, new_search)
    weights = weights_of(grads, new_search[...])
    fisher_rows(prior, grads, new_search, weights, image)
    curve = pair_sums(new_search[me] * image[...])
    for s in range(8):
        payload[s] = jnp.broadcast_to(curve, (8, LANES))
    own[0] = new_solution[me]
    own[1] = new_search[me]
    own[2] = jnp.broadcast_to(norm, (8, LANES))
    values[0] = jnp.broadcast_to(weights_of(grads, new_solution[...]), values.shape[1:])
    values[1] = jnp.broadcast_to(weights, values.shape[1:])


def end_kernel(curves, own, values, scores, solution):
    alpha = own[2] / jnp.sum(curves[...], axis=0)
    done = own[0] + alpha * own[1]
    for j in range(2):
        for c in range(4):
            solution[pl.ds(j, 1), pl.ds(c * LANES, LANES)] = done[j * 4 + c : j * 4 + c + 1]
    total = values.shape[1]
    lane = lax.broadcasted_iota(jnp.int32, (8, LANES), 1)
    table = jnp.zeros((8, LANES), jnp.float32)
    for i in range(total):
        table = jnp.where(lane == i, (values[0, i] + alpha * values[1, i]) / RANK, table)
    for j in range(2):
        scores[pl.ds(j, 1), :] = table[j * 4 : j * 4 + 1, :total]


def call(kernel, shapes, operands, scratch=(), limit=24):
    return pl.pallas_call(
        kernel,
        out_shape=[jax.ShapeDtypeStruct(s, jnp.float32) for s in shapes],
        in_specs=[VMEM] * len(operands),
        out_specs=[VMEM] * len(shapes),
        scratch_shapes=[pltpu.VMEM(s, jnp.float32) for s in scratch],
        compiler_params=pltpu.CompilerParams(vmem_limit_bytes=limit * 2**20),
        name=kernel.__name__,
    )(*operands)


def nearest_first(n, first):
    far = lambda i: abs((i >> 1) - (first >> 1)) + abs((i & 1) - (first & 1))
    return sorted(range(n), key=lambda i: (far(i), i))


ORDER = nearest_first(8, 2)


def flipped(n, bit):
    return [(i, i ^ bit) for i in range(n)]


def per_device(
    train_inputs,
    train_outgrads,
    test_inputs,
    test_outgrads,
    train_counts,
    test_counts,
    proj_in,
    proj_out,
    fisher_prior,
):
    n = 8
    length = train_inputs.shape[1]
    counts = (train_counts, test_counts)
    operands = counts + (
        train_inputs, train_outgrads, test_inputs, test_outgrads, proj_in, proj_out
    )
    near = lambda x: lax.ppermute(x, "tensor", flipped(n, 1))
    next_to = lambda x: lax.ppermute(x, "tensor", flipped(n, 2))
    beyond = lambda x: lax.ppermute(x, "tensor", flipped(n, 4))
    (sent0,) = project_rows([(True, 0, (256,))], operands)
    got0 = near(sent0)
    (sent1,) = project_rows([(True, 256, (256,))], operands, (sent0,))
    got1 = near(sent1)
    kept0, sent2 = project_rows([(False, 0, (256,)), (True, 512, (256,))], operands, (sent1,))
    got2 = near(sent2)
    theirs_a, ours_a = halve(1, [(kept0, 0, got0)])
    half_a = next_to(theirs_a)
    kept1, sent3, sent4 = project_rows(
        [(False, 256, (256,)), (True, 768, (128, 128))], operands, (sent2, theirs_a)
    )
    got3 = near(sent3)
    got4 = near(sent4)
    theirs_b, ours_b = halve(1, [(kept1, 0, got1)])
    half_b = next_to(theirs_b)
    send_a, last_a = halve(2, [(ours_a, 0, half_a)], (theirs_b,))
    whole_a = beyond(send_a)
    kept2, kept3 = project_rows(
        [(False, 512, (256,)), (False, 768, (256,))], operands, (sent4, send_a)
    )
    theirs_c, ours_c = halve(1, [(kept2, 0, got2)], (whole_a,))
    half_c = next_to(theirs_c)
    send_b, last_b = halve(2, [(ours_b, 0, half_b)], (theirs_c,))
    whole_b = beyond(send_b)
    theirs_d, ours_d = halve(1, [(kept3, 0, got3)], (send_b,))
    half_d = next_to(theirs_d)
    theirs_e, ours_e = halve(1, [(kept3, 128, got4)], (theirs_d,))
    half_e = next_to(theirs_e)
    send_c, last_c = halve(2, [(ours_c, 0, half_c)], (theirs_e, whole_b))
    whole_c = beyond(send_c)
    send_d, last_d = halve(2, [(ours_d, 0, half_d)], (send_c,))
    whole_d = beyond(send_d)
    send_e, last_e = halve(2, [(ours_e, 0, half_e)], (send_d,))
    whole_e = beyond(send_e)
    square, prior = gram(
        0, length, counts, (last_a, last_b, last_c), (whole_a, whole_b, whole_c), prior=fisher_prior
    )
    grad = gram(768, length, counts, (last_d, last_e), (whole_d, whole_e), before=square)
    own = lax.all_to_all(grad, "tensor", 0, 0, tiled=True, axis_index_groups=[ORDER])
    other = lax.ppermute(own, "dp", flipped(2, 1))
    per = train_inputs.shape[0]
    state = (8, 8, LANES)
    piece = (8, LANES)
    total = 2 * per
    grads, search, payload = call(
        begin_kernel, [(total, 8, 8, LANES), state, state], (own, other, prior), [piece]
    )
    swap = lambda x: lax.all_to_all(x, "tensor", 0, 0, tiled=True, axis_index_groups=[ORDER])
    solution, residue, search, payload = call(
        first_kernel, [state] * 4, (swap(payload), search, grads, prior), [piece]
    )
    for _ in range(ITERS - 3):
        solution, residue, search, payload = call(
            step_kernel,
            [state] * 4,
            (swap(payload), solution, residue, search, grads, prior),
            [piece],
        )
    ours, payload, values = call(
        last_kernel,
        [(3, 8, LANES), state, (2, total, 8, LANES)],
        (swap(payload), solution, residue, search, grads, prior),
        [state, state, state, piece],
    )
    return tuple(
        call(
            end_kernel,
            [(2, total), (2, fisher_prior.shape[0])],
            (swap(payload), ours, values),
        )
    )


def solution(mesh):
    in_specs = (
        P(("parts", "dp"), None, "tensor"),
        P(("parts", "dp"), None, "tensor"),
        P(("parts", "dp"), None, "tensor"),
        P(("parts", "dp"), None, "tensor"),
        P(("parts", "dp")),
        P(("parts", "dp")),
        P(None, "tensor"),
        P(None, "tensor"),
        P(("parts", "tensor"), None),
    )
    out_specs = (P(("parts", "dp"), None), P(("parts", "dp"), "tensor"))
    body = per_device if mesh.shape["tensor"] == 8 and mesh.shape["dp"] == 2 else plain
    return jax.shard_map(
        body, mesh=mesh, in_specs=in_specs, out_specs=out_specs, check_vma=False
    )
```

```python
import functools
import math

import jax
import jax.numpy as jnp
from jax import lax
from jax.experimental import pallas as pl
from jax.experimental.pallas import tpu as pltpu
from jax.sharding import PartitionSpec as P

RANK = 64
ITERS = 6
LANES = 128
FLOOR = 256
SLOTS = 4
SMALL = 24 * 2**20

HIGH = lax.Precision.HIGHEST
VMEM = pl.BlockSpec(memory_space=pltpu.VMEM)
SMEM = pl.BlockSpec(memory_space=pltpu.SMEM)
ANY = pl.BlockSpec(memory_space=pl.ANY)


def project(data, basis):
    rows = data.reshape(-1, data.shape[-1])
    return lax.dot_general(
        rows, basis, (((1,), (1,)), ((), ())), preferred_element_type=jnp.float32
    )


def outer_sums(left, right, counts, length):
    examples = counts.shape[0]
    left = left.reshape(examples, length, -1)
    right = right.reshape(examples, length, -1)
    live = (jnp.arange(length, dtype=jnp.int32)[None, :] < counts[:, None]).astype(jnp.float32)
    grads = jnp.einsum("etr,ets->ers", left * live[:, :, None], right, precision=HIGH)
    return grads.reshape(examples, -1) * (1.0 / math.sqrt(length))


def plain(
    train_inputs,
    train_outgrads,
    test_inputs,
    test_outgrads,
    train_counts,
    test_counts,
    proj_in,
    proj_out,
    fisher_prior,
):
    length = train_inputs.shape[1]
    left_train = project(train_outgrads, proj_out)
    right_train = project(train_inputs, proj_in)
    left_test = project(test_outgrads, proj_out)
    right_test = project(test_inputs, proj_in)
    left_train, right_train, left_test, right_test = lax.psum(
        (left_train, right_train, left_test, right_test), "tensor"
    )
    train_grads = outer_sums(left_train, right_train, train_counts, length)
    test_grads = outer_sums(left_test, right_test, test_counts, length)
    every_train = lax.all_gather(train_grads, "dp", axis=0, tiled=True)
    total_train = every_train.shape[0]
    own_rows = fisher_prior.shape[0]
    start = lax.axis_index("tensor") * own_rows
    own_train = lax.dynamic_slice_in_dim(every_train, start, own_rows, 1)
    fisher_rows = fisher_prior + jnp.dot(own_train.T, every_train, precision=HIGH) / total_train
    residue = test_grads
    search = test_grads
    solution = jnp.zeros_like(test_grads)
    norm_now = jnp.sum(test_grads * test_grads, axis=1)
    for step in range(ITERS):
        part = lax.dot_general(search, fisher_rows, (((1,), (1,)), ((), ())), precision=HIGH)
        image = lax.all_gather(part, "tensor", axis=1, tiled=True)
        alpha = norm_now / jnp.sum(search * image, axis=1)
        solution = solution + alpha[:, None] * search
        residue = residue - alpha[:, None] * image
        norm_next = jnp.sum(residue * residue, axis=1)
        search = residue + (norm_next / norm_now)[:, None] * search
        norm_now = norm_next
    scores = jnp.dot(solution, every_train.T, precision=HIGH) / RANK
    return (scores, lax.dynamic_slice_in_dim(solution, start, own_rows, 1))


def project_kernel(
    parts, tile, after, train_count, test_count, train_in, train_out, test_in, test_out,
    basis_in, basis_out, *rest,
):
    outs = rest[after : after + sum(len(part[2]) for part in parts)]
    held_in, held_out, near_in, near_out, of_train, of_test, sems, more = rest[after + len(outs) :]
    me = lax.rem(lax.axis_index("tensor"), 2)
    last = train_in.shape[0] // 2
    total = 4 * len(parts)
    dynamic = any(first >= FLOOR for _, first, _ in parts)

    def pick(part, values):
        value = jnp.int32(values[0])
        for g in range(1, len(values)):
            value = jnp.where(part == g, values[g], value)
        return value

    def place(k):
        part = k // 4
        low = pick(part, [int(p[0]) for p in parts]) ^ me
        return lax.rem(k, 4), pl.multiple_of(pick(part, [p[1] for p in parts]), LANES), low

    def live(k):
        if not dynamic:
            return jnp.bool_(True)
        i, row, low = place(k)
        train = of_train[jnp.minimum(2 * i + low, 2 * last - 1)]
        return (jnp.where(i < last, train, of_test[low]) > row) | (k == 0)

    def copies(k, train):
        i, row, low = place(k)
        slot = lax.rem(k, SLOTS)
        rows = pl.ds(row, tile)
        wide, narrow, e = (train_in, train_out, 2 * i + low) if train else (test_in, test_out, low)
        return (
            pltpu.make_async_copy(wide.at[e, rows], held_in.at[slot], sems.at[slot, 0]),
            pltpu.make_async_copy(narrow.at[e, rows], held_out.at[slot], sems.at[slot, 1]),
        )

    def start(k):
        mine = (k < total) & live(k)
        i = lax.rem(k, 4)

        @pl.when(mine & (i < last))
        def _():
            for copy in copies(k, True):
                copy.start()

        @pl.when(mine & (i == last))
        def _():
            for copy in copies(k, False):
                copy.start()

    bases = (
        pltpu.make_async_copy(basis_in, near_in, more.at[0]),
        pltpu.make_async_copy(basis_out, near_out, more.at[1]),
    )
    if dynamic:
        lengths = (
            pltpu.make_async_copy(train_count, of_train, more.at[2]),
            pltpu.make_async_copy(test_count, of_test, more.at[3]),
        )
        for copy in lengths:
            copy.start()
    for copy in copies(jnp.int32(0), True) + bases:
        copy.start()
    if dynamic:
        for copy in lengths:
            copy.wait()

    @pl.loop(1, SLOTS - 1)
    def _(k):
        start(k)

    for copy in bases:
        copy.wait()

    @pl.loop(0, total)
    def _(k):
        i, _, _ = place(k)
        slot = lax.rem(k, SLOTS)
        start(k + SLOTS - 1)

        def keep(rows):
            at = 0
            for g, (_, _, pieces) in enumerate(parts):

                @pl.when(k // 4 == g)
                def _():
                    done = 0
                    for n, size in enumerate(pieces):
                        outs[at + n][i] = rows[done : done + size]
                        done += size

                at += len(pieces)

        def make():
            for copy in copies(k, False):
                copy.wait()
            dims = (((1,), (1,)), ((), ()))
            left = lax.dot_general(
                held_out[slot], near_out[...], dims, preferred_element_type=jnp.float32
            )
            right = lax.dot_general(
                held_in[slot], near_in[...], dims, preferred_element_type=jnp.float32
            )
            keep(jnp.concatenate([left, right], axis=1))

        if dynamic:
            alive = live(k)
            pl.when(alive)(make)

            @pl.when(jnp.logical_not(alive))
            def _():
                keep(jnp.zeros((tile, LANES), jnp.float32))

        else:
            make()


def in_hbm(arrays):
    return [pltpu.with_memory_space_constraint(x, pltpu.HBM) for x in arrays]


def project_rows(parts, operands, after=()):
    wide, narrow, basis_in, basis_out = operands[2], operands[3], operands[6], operands[7]
    tile = sum(parts[0][2])
    sizes = [size for part in parts for size in part[2]]
    rows = 4 * sum(sizes)
    depth = wide.shape[2] + narrow.shape[2]
    return pl.pallas_call(
        functools.partial(project_kernel, parts, tile, len(after)),
        out_shape=[pltpu.VMEM((4, size, LANES), jnp.float32) for size in sizes],
        in_specs=[ANY] * (len(operands) + len(after)),
        out_specs=[VMEM] * len(sizes),
        scratch_shapes=[
            pltpu.VMEM((SLOTS, tile, wide.shape[2]), wide.dtype),
            pltpu.VMEM((SLOTS, tile, narrow.shape[2]), narrow.dtype),
            pltpu.VMEM(basis_in.shape, basis_in.dtype),
            pltpu.VMEM(basis_out.shape, basis_out.dtype),
            pltpu.SMEM(operands[0].shape, jnp.int32),
            pltpu.SMEM(operands[1].shape, jnp.int32),
            pltpu.SemaphoreType.DMA((SLOTS, 2)),
            pltpu.SemaphoreType.DMA((4,)),
        ],
        compiler_params=pltpu.CompilerParams(vmem_limit_bytes=SMALL),
        cost_estimate=pl.CostEstimate(
            flops=2 * rows * depth * RANK, bytes_accessed=rows * depth * 2, transcendentals=0
        ),
        name="project_" + "_".join(f"{'send' if p[0] else 'keep'}{p[1]}" for p in parts),
    )(*in_hbm(operands), *after)


def halve_kernel(offsets, bit, *refs):
    pairs = len(offsets)
    kept, got, (theirs, ours) = refs[:pairs], refs[pairs : 2 * pairs], refs[-2:]
    mine = (lax.axis_index("tensor") >> bit) & 1
    at = 0
    for offset, base, piece in zip(offsets, kept, got):
        rows = piece.shape[1]
        here, there = pl.ds(offset, rows), pl.ds(at, rows)
        for h in range(theirs.shape[0]):
            give = 2 * h + 1 - mine if bit == 1 else 1 - mine
            take = 2 * h + mine if bit == 1 else mine
            theirs[h, there, :] = base[give, here, :] + piece[give, :, :]
            ours[h, there, :] = base[take, here, :] + piece[take, :, :]
        at += rows


def halve(bit, pairs, after=()):
    kept, offsets, got = zip(*pairs)
    rows = sum(piece.shape[1] for piece in got)
    shape = pltpu.VMEM((kept[0].shape[0] // 2, rows, LANES), jnp.float32)
    return pl.pallas_call(
        functools.partial(halve_kernel, offsets, bit),
        out_shape=[shape, shape],
        in_specs=[VMEM] * (2 * len(pairs)) + [ANY] * len(after),
        out_specs=[VMEM, VMEM],
        compiler_params=pltpu.CompilerParams(vmem_limit_bytes=SMALL),
        name=f"halve{bit}",
    )(*kept, *got, *after)


def gram_kernel(first, pieces, length, final, *rest):
    ours, got = rest[:pieces], rest[pieces : 2 * pieces]
    rest = rest[2 * pieces :]
    if final:
        before, limit, out, held = rest
        count = limit[:1, :]
    else:
        train_count, test_count, prior, out, near, limit, of_train, of_test, sems, more = rest
        fetch = pltpu.make_async_copy(prior, near, more)
        fetch.start()
        me = lax.axis_index("tensor")
        train = train_count.shape[0]
        lengths = (
            pltpu.make_async_copy(train_count, of_train, sems.at[0]),
            pltpu.make_async_copy(test_count, of_test, sems.at[1]),
        )
        for copy in lengths:
            copy.start()
        for copy in lengths:
            copy.wait()
        count = jnp.where(
            me < train,
            of_train[jnp.minimum(me, train - 1)],
            of_test[jnp.maximum(me - train, 0)],
        )
        limit[...] = jnp.full(limit.shape, count, jnp.int32)
    total = before[...] if final else jnp.zeros((RANK, RANK), jnp.float32)
    for a, b in zip(ours, got):
        rows = a[0] + b[0]
        live = lax.broadcasted_iota(jnp.int32, rows.shape, 0) + first < count
        rows = jnp.where(live, rows, 0.0)
        total = total + lax.dot_general(
            rows[:, :RANK], rows[:, RANK:], (((0,), (0,)), ((), ())), precision=HIGH,
            preferred_element_type=jnp.float32,
        )
        first += rows.shape[0]
    if not final:
        out[...] = total
        fetch.wait()
        return
    held[...] = total * (1.0 / math.sqrt(length))
    half = RANK // 2
    grad = jnp.concatenate(
        [held[pl.ds(0, half, stride=2), :], held[pl.ds(1, half, stride=2), :]], axis=1
    )
    for i in range(out.shape[0]):
        out[i] = grad


def gram(first, length, ours, got, counts=None, prior=None, before=None):
    final = before is not None
    if final:
        others, other_specs = before, [VMEM, VMEM]
        out_shape = jax.ShapeDtypeStruct((8, RANK // 2, LANES), jnp.float32)
        scratch = [pltpu.VMEM((RANK, RANK), jnp.float32)]
    else:
        others, other_specs = in_hbm(counts + (prior,)), [ANY, ANY, ANY]
        out_shape = [
            jax.ShapeDtypeStruct((RANK, RANK), jnp.float32),
            pltpu.VMEM(prior.shape, prior.dtype),
            jax.ShapeDtypeStruct((8, LANES), jnp.int32),
        ]
        scratch = [pltpu.SMEM(c.shape, jnp.int32) for c in counts]
        scratch += [pltpu.SemaphoreType.DMA((2,)), pltpu.SemaphoreType.DMA]
    return pl.pallas_call(
        functools.partial(gram_kernel, first, len(ours), length, final),
        out_shape=out_shape,
        in_specs=[VMEM] * (2 * len(ours)) + other_specs,
        out_specs=VMEM if final else [VMEM] * 3,
        scratch_shapes=scratch,
        compiler_params=pltpu.CompilerParams(vmem_limit_bytes=SMALL),
        name="gram_end" if final else "gram_begin",
    )(*ours, *got, *others)


def pair_sums(x):
    x = jnp.sum(x, axis=-1, keepdims=True)
    upper = lax.broadcasted_iota(jnp.int32, x.shape, x.ndim - 2) < 4
    first = jnp.sum(jnp.where(upper, x, 0.0), axis=-2, keepdims=True)
    second = jnp.sum(jnp.where(upper, 0.0, x), axis=-2, keepdims=True)
    return jnp.where(upper, first, second)


def inner(a, b):
    return pair_sums(jnp.sum(a * b, axis=0))


def weights_of(grads, vector):
    return pair_sums(
        jnp.stack([jnp.sum(grads[i] * vector, axis=0) for i in range(grads.shape[0])])
    )


def fisher_rows(prior, grads, vector, weights, image):
    me = lax.axis_index("tensor")

    @pl.loop(0, prior.shape[0] // LANES)
    def _(block):
        rows = pl.ds(pl.multiple_of(block * LANES, LANES), LANES)
        sums = [jnp.zeros((LANES, LANES), jnp.float32)] * 2
        for c in range(prior.shape[1] // LANES):
            piece = prior[rows, pl.ds(c * LANES, LANES)]
            for j in range(2):
                sums[j] = sums[j] + piece * vector[c // 4, pl.ds(j * 4 + c % 4, 1), :]
        for j in range(2):
            line = jnp.sum(sums[j].T, axis=0, keepdims=True)
            image[pl.ds(j * 4 + block, 1), :] = line

    if grads is None:
        return
    total = grads.shape[0]
    low = weights[0] * grads[0, me]
    for i in range(1, total):
        low = low + weights[i] * grads[i, me]
    image[...] = image[...] + low * (1.0 / total)


def begin_kernel(own, prior, search, payload, image):
    first = own.shape[0] - 2
    for j in range(2):
        for s in range(8):
            search[s, pl.ds(j * 4, 4), :] = own[ORDER.index(first + j), pl.ds(s * 4, 4), :]
    fisher_rows(prior, None, search, None, image)
    for s in range(8):
        payload[s] = image[...]


def in_order(images):
    return jnp.stack([images[ORDER.index(s)] for s in range(8)])


def advance(first, image, solution, residue, search, new_solution, new_residue, new_search):
    old = search[...]
    rest = old if first else residue[...]
    norm = inner(rest, rest)
    alpha = norm / inner(old, image)
    new_solution[...] = alpha * old if first else solution[...] + alpha * old
    rest = rest - alpha * image
    new_residue[...] = rest
    norm_next = inner(rest, rest)
    new_search[...] = rest + (norm_next / norm) * old
    return norm_next


def first_kernel(
    images, search, own, other, prior,
    new_solution, new_residue, new_search, payload, grads, image,
):
    me = lax.axis_index("dp")
    total = grads.shape[0]
    per = total // 2
    for i in range(per):
        at = ORDER.index(i)
        for s in range(8):
            for half in range(2):
                there, here = pl.ds(half * 4, 4), pl.ds(s * 4, 4)
                grads[me * per + i, s, there, :] = own[at, here, :]
                grads[(1 - me) * per + i, s, there, :] = other[at, here, :]
    weights = weights_of(grads, search[...])
    low = weights[0] * grads[0]
    for i in range(1, total):
        low = low + weights[i] * grads[i]
    whole = in_order(images) + low * (1.0 / total)
    advance(True, whole, None, None, search, new_solution, new_residue, new_search)
    fisher_rows(prior, grads, new_search, weights_of(grads, new_search[...]), image)
    for s in range(8):
        payload[s] = image[...]


def step_kernel(
    images, solution, residue, search, grads, prior,
    new_solution, new_residue, new_search, payload, image,
):
    advance(False, in_order(images), solution, residue, search, new_solution, new_residue, new_search)
    fisher_rows(prior, grads, new_search, weights_of(grads, new_search[...]), image)
    for s in range(8):
        payload[s] = image[...]


def last_kernel(
    images, solution, residue, search, grads, prior,
    own, payload, values, new_solution, new_residue, new_search, image,
):
    me = lax.axis_index("tensor")
    norm = advance(False, in_order(images), solution, residue, search, new_solution, new_residue, new_search)
    weights = weights_of(grads, new_search[...])
    fisher_rows(prior, grads, new_search, weights, image)
    curve = pair_sums(new_search[me] * image[...])
    for s in range(8):
        payload[s] = jnp.broadcast_to(curve, (8, LANES))
    own[0] = new_solution[me]
    own[1] = new_search[me]
    own[2] = jnp.broadcast_to(norm, (8, LANES))
    values[0] = jnp.broadcast_to(weights_of(grads, new_solution[...]), values.shape[1:])
    values[1] = jnp.broadcast_to(weights, values.shape[1:])


def end_kernel(curves, own, values, scores, solution):
    alpha = own[2] / jnp.sum(curves[...], axis=0)
    done = own[0] + alpha * own[1]
    for j in range(2):
        for c in range(4):
            solution[pl.ds(j, 1), pl.ds(c * LANES, LANES)] = done[j * 4 + c : j * 4 + c + 1]
    total = values.shape[1]
    lane = lax.broadcasted_iota(jnp.int32, (8, LANES), 1)
    table = jnp.zeros((8, LANES), jnp.float32)
    for i in range(total):
        table = jnp.where(lane == i, (values[0, i] + alpha * values[1, i]) / RANK, table)
    for j in range(2):
        scores[pl.ds(j, 1), :] = table[j * 4 : j * 4 + 1, :total]


def call(kernel, shapes, operands, scratch=(), limit=24):
    return pl.pallas_call(
        kernel,
        out_shape=[jax.ShapeDtypeStruct(s, jnp.float32) for s in shapes],
        in_specs=[VMEM] * len(operands),
        out_specs=[VMEM] * len(shapes),
        scratch_shapes=[pltpu.VMEM(s, jnp.float32) for s in scratch],
        compiler_params=pltpu.CompilerParams(vmem_limit_bytes=limit * 2**20),
        name=kernel.__name__,
    )(*operands)


def nearest_first(n, first):
    far = lambda i: abs((i >> 1) - (first >> 1)) + abs((i & 1) - (first & 1))
    return sorted(range(n), key=lambda i: (far(i), i))


ORDER = nearest_first(8, 2)


def flipped(n, bit):
    return [(i, i ^ bit) for i in range(n)]


def per_device(
    train_inputs,
    train_outgrads,
    test_inputs,
    test_outgrads,
    train_counts,
    test_counts,
    proj_in,
    proj_out,
    fisher_prior,
):
    n = 8
    length = train_inputs.shape[1]
    counts = (train_counts, test_counts)
    operands = counts + (
        train_inputs, train_outgrads, test_inputs, test_outgrads, proj_in, proj_out
    )
    near = lambda x: lax.ppermute(x, "tensor", flipped(n, 1))
    next_to = lambda x: lax.ppermute(x, "tensor", flipped(n, 2))
    beyond = lambda x: lax.ppermute(x, "tensor", flipped(n, 4))
    (sent0,) = project_rows([(True, 0, (256,))], operands)
    got0 = near(sent0)
    (sent1,) = project_rows([(True, 256, (256,))], operands, (sent0,))
    got1 = near(sent1)
    kept0, sent2 = project_rows([(False, 0, (256,)), (True, 512, (256,))], operands, (sent1,))
    got2 = near(sent2)
    theirs_a, ours_a = halve(1, [(kept0, 0, got0)])
    half_a = next_to(theirs_a)
    kept1, sent3, sent4 = project_rows(
        [(False, 256, (256,)), (True, 768, (128, 128))], operands, (sent2, theirs_a)
    )
    got3 = near(sent3)
    got4 = near(sent4)
    theirs_b, ours_b = halve(1, [(kept1, 0, got1)])
    half_b = next_to(theirs_b)
    send_a, last_a = halve(2, [(ours_a, 0, half_a)], (theirs_b,))
    whole_a = beyond(send_a)
    (kept2,) = project_rows([(False, 512, (256,))], operands, (sent4, send_a))
    theirs_c, ours_c = halve(1, [(kept2, 0, got2)], (whole_a,))
    half_c = next_to(theirs_c)
    send_b, last_b = halve(2, [(ours_b, 0, half_b)], (theirs_c,))
    whole_b = beyond(send_b)
    (kept3,) = project_rows([(False, 768, (256,))], operands, (kept2, send_b))
    theirs_d, ours_d = halve(1, [(kept3, 0, got3)], (send_b,))
    half_d = next_to(theirs_d)
    theirs_e, ours_e = halve(1, [(kept3, 128, got4)], (theirs_d,))
    half_e = next_to(theirs_e)
    send_c, last_c = halve(2, [(ours_c, 0, half_c)], (theirs_e, whole_b))
    whole_c = beyond(send_c)
    send_d, last_d = halve(2, [(ours_d, 0, half_d)], (send_c,))
    whole_d = beyond(send_d)
    send_e, last_e = halve(2, [(ours_e, 0, half_e)], (send_d,))
    whole_e = beyond(send_e)
    square, prior, limit = gram(
        0, length, (last_a, last_b, last_c), (whole_a, whole_b, whole_c), counts, fisher_prior
    )
    grad = gram(768, length, (last_d, last_e), (whole_d, whole_e), before=(square, limit))
    own = lax.all_to_all(grad, "tensor", 0, 0, tiled=True, axis_index_groups=[ORDER])
    other = lax.ppermute(own, "dp", flipped(2, 1))
    per = train_inputs.shape[0]
    state = (8, 8, LANES)
    piece = (8, LANES)
    total = 2 * per
    search, payload = call(begin_kernel, [state, state], (own, prior), [piece])
    swap = lambda x: lax.all_to_all(x, "tensor", 0, 0, tiled=True, axis_index_groups=[ORDER])
    solution, residue, search, payload, grads = call(
        first_kernel,
        [state] * 4 + [(total,) + state],
        (swap(payload), search, own, other, prior),
        [piece],
    )
    for _ in range(ITERS - 3):
        solution, residue, search, payload = call(
            step_kernel,
            [state] * 4,
            (swap(payload), solution, residue, search, grads, prior),
            [piece],
        )
    ours, payload, values = call(
        last_kernel,
        [(3, 8, LANES), state, (2, total, 8, LANES)],
        (swap(payload), solution, residue, search, grads, prior),
        [state, state, state, piece],
    )
    return tuple(
        call(
            end_kernel,
            [(2, total), (2, fisher_prior.shape[0])],
            (swap(payload), ours, values),
        )
    )


def solution(mesh):
    in_specs = (
        P(("parts", "dp"), None, "tensor"),
        P(("parts", "dp"), None, "tensor"),
        P(("parts", "dp"), None, "tensor"),
        P(("parts", "dp"), None, "tensor"),
        P(("parts", "dp")),
        P(("parts", "dp")),
        P(None, "tensor"),
        P(None, "tensor"),
        P(("parts", "tensor"), None),
    )
    out_specs = (P(("parts", "dp"), None), P(("parts", "dp"), "tensor"))
    body = per_device if mesh.shape["tensor"] == 8 and mesh.shape["dp"] == 2 else plain
    return jax.shard_map(
        body, mesh=mesh, in_specs=in_specs, out_specs=out_specs, check_vma=False
    )
```

```python
import functools
import math

import jax
import jax.numpy as jnp
from jax import lax
from jax.experimental import pallas as pl
from jax.experimental.pallas import tpu as pltpu
from jax.sharding import PartitionSpec as P

RANK = 64
ITERS = 6
LANES = 128
FLOOR = 256
SLOTS = 3
SMALL = 24 * 2**20

HIGH = lax.Precision.HIGHEST
VMEM = pl.BlockSpec(memory_space=pltpu.VMEM)
SMEM = pl.BlockSpec(memory_space=pltpu.SMEM)
ANY = pl.BlockSpec(memory_space=pl.ANY)


def project(data, basis):
    rows = data.reshape(-1, data.shape[-1])
    return lax.dot_general(
        rows, basis, (((1,), (1,)), ((), ())), preferred_element_type=jnp.float32
    )


def outer_sums(left, right, counts, length):
    examples = counts.shape[0]
    left = left.reshape(examples, length, -1)
    right = right.reshape(examples, length, -1)
    live = (jnp.arange(length, dtype=jnp.int32)[None, :] < counts[:, None]).astype(jnp.float32)
    grads = jnp.einsum("etr,ets->ers", left * live[:, :, None], right, precision=HIGH)
    return grads.reshape(examples, -1) * (1.0 / math.sqrt(length))


def plain(
    train_inputs,
    train_outgrads,
    test_inputs,
    test_outgrads,
    train_counts,
    test_counts,
    proj_in,
    proj_out,
    fisher_prior,
):
    length = train_inputs.shape[1]
    left_train = project(train_outgrads, proj_out)
    right_train = project(train_inputs, proj_in)
    left_test = project(test_outgrads, proj_out)
    right_test = project(test_inputs, proj_in)
    left_train, right_train, left_test, right_test = lax.psum(
        (left_train, right_train, left_test, right_test), "tensor"
    )
    train_grads = outer_sums(left_train, right_train, train_counts, length)
    test_grads = outer_sums(left_test, right_test, test_counts, length)
    every_train = lax.all_gather(train_grads, "dp", axis=0, tiled=True)
    total_train = every_train.shape[0]
    own_rows = fisher_prior.shape[0]
    start = lax.axis_index("tensor") * own_rows
    own_train = lax.dynamic_slice_in_dim(every_train, start, own_rows, 1)
    fisher_rows = fisher_prior + jnp.dot(own_train.T, every_train, precision=HIGH) / total_train
    residue = test_grads
    search = test_grads
    solution = jnp.zeros_like(test_grads)
    norm_now = jnp.sum(test_grads * test_grads, axis=1)
    for step in range(ITERS):
        part = lax.dot_general(search, fisher_rows, (((1,), (1,)), ((), ())), precision=HIGH)
        image = lax.all_gather(part, "tensor", axis=1, tiled=True)
        alpha = norm_now / jnp.sum(search * image, axis=1)
        solution = solution + alpha[:, None] * search
        residue = residue - alpha[:, None] * image
        norm_next = jnp.sum(residue * residue, axis=1)
        search = residue + (norm_next / norm_now)[:, None] * search
        norm_now = norm_next
    scores = jnp.dot(solution, every_train.T, precision=HIGH) / RANK
    return (scores, lax.dynamic_slice_in_dim(solution, start, own_rows, 1))


def project_kernel(
    parts, tile, after, train_count, test_count, train_in, train_out, test_in, test_out,
    basis_in, basis_out, *rest,
):
    outs = rest[after : after + sum(len(part[2]) for part in parts)]
    held, basis, of_train, of_test, sems, more = rest[after + len(outs) :]
    width, depth = basis_in.shape[1], basis.shape[1]
    front, back = pl.ds(0, width), pl.ds(width, depth - width)
    upper, lower = pl.ds(0, RANK), pl.ds(RANK, RANK)
    me = lax.rem(lax.axis_index("tensor"), 2)
    last = train_in.shape[0] // 2
    total = 4 * len(parts)
    always = [first <= FLOOR for _, first, _ in parts]
    dynamic = not all(always)

    def pick(part, values):
        value = jnp.int32(values[0])
        for g in range(1, len(values)):
            value = jnp.where(part == g, values[g], value)
        return value

    def place(k):
        part = k // 4
        low = pick(part, [int(p[0]) for p in parts]) ^ me
        return lax.rem(k, 4), pl.multiple_of(pick(part, [p[1] for p in parts]), LANES), low

    def live(k):
        if not dynamic:
            return jnp.bool_(True)
        i, row, low = place(k)
        train = of_train[jnp.minimum(2 * i + low, 2 * last - 1)]
        kept = (pick(k // 4, [int(flag) for flag in always]) == 1) | (k == 0)
        return (jnp.where(i < last, train, of_test[low]) > row) | kept

    def copies(k, train):
        i, row, low = place(k)
        slot = lax.rem(k, SLOTS)
        rows = pl.ds(row, tile)
        wide, narrow, e = (train_in, train_out, 2 * i + low) if train else (test_in, test_out, low)
        return (
            pltpu.make_async_copy(wide.at[e, rows], held.at[slot, :, front], sems.at[slot, 0]),
            pltpu.make_async_copy(narrow.at[e, rows], held.at[slot, :, back], sems.at[slot, 1]),
        )

    def start(k, sure=False):
        mine = k < total if sure else (k < total) & live(k)
        i = lax.rem(k, 4)

        @pl.when(mine & (i < last))
        def _():
            for copy in copies(k, True):
                copy.start()

        @pl.when(mine & (i == last))
        def _():
            for copy in copies(k, False):
                copy.start()

    bases = (
        pltpu.make_async_copy(basis_in, basis.at[lower, front], more.at[0]),
        pltpu.make_async_copy(basis_out, basis.at[upper, back], more.at[1]),
    )
    if dynamic:
        lengths = (
            pltpu.make_async_copy(train_count, of_train, more.at[2]),
            pltpu.make_async_copy(test_count, of_test, more.at[3]),
        )
        for copy in lengths:
            copy.start()
    for copy in copies(jnp.int32(0), True) + bases:
        copy.start()
    basis[upper, front] = jnp.zeros((RANK, width), basis.dtype)
    basis[lower, back] = jnp.zeros((RANK, depth - width), basis.dtype)
    if dynamic and not always[0]:
        for copy in lengths:
            copy.wait()

    @pl.loop(1, SLOTS - 1)
    def _(k):
        start(k, always[0])

    if dynamic and always[0]:
        for copy in lengths:
            copy.wait()
    for copy in bases:
        copy.wait()

    @pl.loop(0, total)
    def _(k):
        i, _, _ = place(k)
        slot = lax.rem(k, SLOTS)
        start(k + SLOTS - 1)

        def keep(rows):
            at = 0
            for g, (_, _, pieces) in enumerate(parts):

                @pl.when(k // 4 == g)
                def _():
                    done = 0
                    for n, size in enumerate(pieces):
                        outs[at + n][i] = rows[done : done + size]
                        done += size

                at += len(pieces)

        def make():
            for copy in copies(k, False):
                copy.wait()
            keep(
                lax.dot_general(
                    held[slot], basis[...], (((1,), (1,)), ((), ())),
                    preferred_element_type=jnp.float32,
                )
            )

        if dynamic:
            alive = live(k)
            pl.when(alive)(make)

            @pl.when(jnp.logical_not(alive))
            def _():
                keep(jnp.zeros((tile, LANES), jnp.float32))

        else:
            make()


def in_hbm(arrays):
    return [pltpu.with_memory_space_constraint(x, pltpu.HBM) for x in arrays]


def project_rows(parts, operands, after=()):
    wide, narrow, basis_in, basis_out = operands[2], operands[3], operands[6], operands[7]
    tile = sum(parts[0][2])
    sizes = [size for part in parts for size in part[2]]
    rows = 4 * sum(sizes)
    depth = wide.shape[2] + narrow.shape[2]
    return pl.pallas_call(
        functools.partial(project_kernel, parts, tile, len(after)),
        out_shape=[pltpu.VMEM((4, size, LANES), jnp.float32) for size in sizes],
        in_specs=[ANY] * (len(operands) + len(after)),
        out_specs=[VMEM] * len(sizes),
        scratch_shapes=[
            pltpu.VMEM((SLOTS, tile, depth), wide.dtype),
            pltpu.VMEM((2 * RANK, depth), basis_in.dtype),
            pltpu.SMEM(operands[0].shape, jnp.int32),
            pltpu.SMEM(operands[1].shape, jnp.int32),
            pltpu.SemaphoreType.DMA((SLOTS, 2)),
            pltpu.SemaphoreType.DMA((4,)),
        ],
        compiler_params=pltpu.CompilerParams(vmem_limit_bytes=SMALL),
        cost_estimate=pl.CostEstimate(
            flops=2 * rows * depth * RANK, bytes_accessed=rows * depth * 2, transcendentals=0
        ),
        name="project_" + "_".join(f"{'send' if p[0] else 'keep'}{p[1]}" for p in parts),
    )(*in_hbm(operands), *after)


def halve_kernel(offsets, bit, *refs):
    pairs = len(offsets)
    kept, got, (theirs, ours) = refs[:pairs], refs[pairs : 2 * pairs], refs[-2:]
    mine = (lax.axis_index("tensor") >> bit) & 1
    at = 0
    for offset, base, piece in zip(offsets, kept, got):
        rows = piece.shape[1]
        here, there = pl.ds(offset, rows), pl.ds(at, rows)
        for h in range(theirs.shape[0]):
            give = 2 * h + 1 - mine if bit == 1 else 1 - mine
            take = 2 * h + mine if bit == 1 else mine
            theirs[h, there, :] = base[give, here, :] + piece[give, :, :]
            ours[h, there, :] = base[take, here, :] + piece[take, :, :]
        at += rows


def halve(bit, pairs, after=()):
    kept, offsets, got = zip(*pairs)
    rows = sum(piece.shape[1] for piece in got)
    shape = pltpu.VMEM((kept[0].shape[0] // 2, rows, LANES), jnp.float32)
    return pl.pallas_call(
        functools.partial(halve_kernel, offsets, bit),
        out_shape=[shape, shape],
        in_specs=[VMEM] * (2 * len(pairs)) + [ANY] * len(after),
        out_specs=[VMEM, VMEM],
        compiler_params=pltpu.CompilerParams(vmem_limit_bytes=SMALL),
        name=f"halve{bit}",
    )(*kept, *got, *after)


def gram_kernel(first, pieces, length, final, *rest):
    ours, got = rest[:pieces], rest[pieces : 2 * pieces]
    rest = rest[2 * pieces :]
    if final:
        before, limit, out, held = rest
        count = limit[:1, :]
    else:
        train_count, test_count, prior, out, near, limit, of_train, of_test, sems, more = rest
        fetch = pltpu.make_async_copy(prior, near, more)
        fetch.start()
        me = lax.axis_index("tensor")
        train = train_count.shape[0]
        lengths = (
            pltpu.make_async_copy(train_count, of_train, sems.at[0]),
            pltpu.make_async_copy(test_count, of_test, sems.at[1]),
        )
        for copy in lengths:
            copy.start()
        for copy in lengths:
            copy.wait()
        count = jnp.where(
            me < train,
            of_train[jnp.minimum(me, train - 1)],
            of_test[jnp.maximum(me - train, 0)],
        )
        limit[...] = jnp.full(limit.shape, count, jnp.int32)
    total = before[...] if final else jnp.zeros((RANK, RANK), jnp.float32)
    for a, b in zip(ours, got):
        rows = a[0] + b[0]
        live = lax.broadcasted_iota(jnp.int32, rows.shape, 0) + first < count
        rows = jnp.where(live, rows, 0.0)
        total = total + lax.dot_general(
            rows[:, :RANK], rows[:, RANK:], (((0,), (0,)), ((), ())), precision=HIGH,
            preferred_element_type=jnp.float32,
        )
        first += rows.shape[0]
    if not final:
        out[...] = total
        fetch.wait()
        return
    held[...] = total * (1.0 / math.sqrt(length))
    half = RANK // 2
    grad = jnp.concatenate(
        [held[pl.ds(0, half, stride=2), :], held[pl.ds(1, half, stride=2), :]], axis=1
    )
    for i in range(out.shape[0]):
        out[i] = grad


def gram(first, length, ours, got, counts=None, prior=None, before=None):
    final = before is not None
    if final:
        others, other_specs = before, [VMEM, VMEM]
        out_shape = jax.ShapeDtypeStruct((8, RANK // 2, LANES), jnp.float32)
        scratch = [pltpu.VMEM((RANK, RANK), jnp.float32)]
    else:
        others, other_specs = in_hbm(counts + (prior,)), [ANY, ANY, ANY]
        out_shape = [
            jax.ShapeDtypeStruct((RANK, RANK), jnp.float32),
            pltpu.VMEM(prior.shape, prior.dtype),
            jax.ShapeDtypeStruct((8, LANES), jnp.int32),
        ]
        scratch = [pltpu.SMEM(c.shape, jnp.int32) for c in counts]
        scratch += [pltpu.SemaphoreType.DMA((2,)), pltpu.SemaphoreType.DMA]
    return pl.pallas_call(
        functools.partial(gram_kernel, first, len(ours), length, final),
        out_shape=out_shape,
        in_specs=[VMEM] * (2 * len(ours)) + other_specs,
        out_specs=VMEM if final else [VMEM] * 3,
        scratch_shapes=scratch,
        compiler_params=pltpu.CompilerParams(vmem_limit_bytes=SMALL),
        name="gram_end" if final else "gram_begin",
    )(*ours, *got, *others)


def pair_sums(x):
    x = jnp.sum(x, axis=-1, keepdims=True)
    upper = lax.broadcasted_iota(jnp.int32, x.shape, x.ndim - 2) < 4
    first = jnp.sum(jnp.where(upper, x, 0.0), axis=-2, keepdims=True)
    second = jnp.sum(jnp.where(upper, 0.0, x), axis=-2, keepdims=True)
    return jnp.where(upper, first, second)


def inner(a, b):
    return pair_sums(jnp.sum(a * b, axis=0))


def weights_of(grads, vector):
    return pair_sums(
        jnp.stack([jnp.sum(grads[i] * vector, axis=0) for i in range(grads.shape[0])])
    )


def fisher_rows(prior, grads, vector, weights, image):
    me = lax.axis_index("tensor")

    @pl.loop(0, prior.shape[0] // LANES, unroll=2)
    def _(block):
        rows = pl.ds(pl.multiple_of(block * LANES, LANES), LANES)
        sums = [jnp.zeros((LANES, LANES), jnp.float32)] * 2
        for c in range(prior.shape[1] // LANES):
            piece = prior[rows, pl.ds(c * LANES, LANES)]
            for j in range(2):
                sums[j] = sums[j] + piece * vector[c // 4, pl.ds(j * 4 + c % 4, 1), :]
        for j in range(2):
            line = jnp.sum(sums[j].T, axis=0, keepdims=True)
            image[pl.ds(j * 4 + block, 1), :] = line

    if grads is None:
        return
    total = grads.shape[0]
    low = weights[0] * grads[0, me]
    for i in range(1, total):
        low = low + weights[i] * grads[i, me]
    image[...] = image[...] + low * (1.0 / total)


def begin_kernel(own, prior, search, payload, image):
    first = own.shape[0] - 2
    for j in range(2):
        for s in range(8):
            search[s, pl.ds(j * 4, 4), :] = own[ORDER.index(first + j), pl.ds(s * 4, 4), :]
    fisher_rows(prior, None, search, None, image)
    for s in range(8):
        payload[s] = image[...]


def in_order(images):
    return jnp.stack([images[ORDER.index(s)] for s in range(8)])


def advance(first, image, solution, residue, search, new_solution, new_residue, new_search):
    old = search[...]
    rest = old if first else residue[...]
    norm = inner(rest, rest)
    alpha = norm / inner(old, image)
    new_solution[...] = alpha * old if first else solution[...] + alpha * old
    rest = rest - alpha * image
    new_residue[...] = rest
    norm_next = inner(rest, rest)
    new_search[...] = rest + (norm_next / norm) * old
    return norm_next


def first_kernel(
    images, search, own, other, prior,
    new_solution, new_residue, new_search, payload, grads, image,
):
    me = lax.axis_index("dp")
    total = grads.shape[0]
    per = total // 2
    for i in range(per):
        at = ORDER.index(i)
        for s in range(8):
            for half in range(2):
                there, here = pl.ds(half * 4, 4), pl.ds(s * 4, 4)
                grads[me * per + i, s, there, :] = own[at, here, :]
                grads[(1 - me) * per + i, s, there, :] = other[at, here, :]
    weights = weights_of(grads, search[...])
    low = weights[0] * grads[0]
    for i in range(1, total):
        low = low + weights[i] * grads[i]
    whole = in_order(images) + low * (1.0 / total)
    advance(True, whole, None, None, search, new_solution, new_residue, new_search)
    fisher_rows(prior, grads, new_search, weights_of(grads, new_search[...]), image)
    for s in range(8):
        payload[s] = image[...]


def step_kernel(
    images, solution, residue, search, grads, prior,
    new_solution, new_residue, new_search, payload, image,
):
    advance(False, in_order(images), solution, residue, search, new_solution, new_residue, new_search)
    fisher_rows(prior, grads, new_search, weights_of(grads, new_search[...]), image)
    for s in range(8):
        payload[s] = image[...]


def last_kernel(
    images, solution, residue, search, grads, prior,
    own, payload, values, new_solution, new_residue, new_search, image,
):
    me = lax.axis_index("tensor")
    norm = advance(False, in_order(images), solution, residue, search, new_solution, new_residue, new_search)
    weights = weights_of(grads, new_search[...])
    fisher_rows(prior, grads, new_search, weights, image)
    curve = pair_sums(new_search[me] * image[...])
    for s in range(8):
        payload[s] = jnp.broadcast_to(curve, (8, LANES))
    own[0] = new_solution[me]
    own[1] = new_search[me]
    own[2] = jnp.broadcast_to(norm, (8, LANES))
    values[0] = jnp.broadcast_to(weights_of(grads, new_solution[...]), values.shape[1:])
    values[1] = jnp.broadcast_to(weights, values.shape[1:])


def end_kernel(curves, own, values, scores, solution):
    alpha = own[2] / jnp.sum(curves[...], axis=0)
    done = own[0] + alpha * own[1]
    for j in range(2):
        for c in range(4):
            solution[pl.ds(j, 1), pl.ds(c * LANES, LANES)] = done[j * 4 + c : j * 4 + c + 1]
    total = values.shape[1]
    lane = lax.broadcasted_iota(jnp.int32, (8, LANES), 1)
    table = jnp.zeros((8, LANES), jnp.float32)
    for i in range(total):
        table = jnp.where(lane == i, (values[0, i] + alpha * values[1, i]) / RANK, table)
    for j in range(2):
        scores[pl.ds(j, 1), :] = table[j * 4 : j * 4 + 1, :total]


def call(kernel, shapes, operands, scratch=(), limit=24):
    return pl.pallas_call(
        kernel,
        out_shape=[jax.ShapeDtypeStruct(s, jnp.float32) for s in shapes],
        in_specs=[VMEM] * len(operands),
        out_specs=[VMEM] * len(shapes),
        scratch_shapes=[pltpu.VMEM(s, jnp.float32) for s in scratch],
        compiler_params=pltpu.CompilerParams(vmem_limit_bytes=limit * 2**20),
        name=kernel.__name__,
    )(*operands)


def nearest_first(n, first):
    far = lambda i: abs((i >> 1) - (first >> 1)) + abs((i & 1) - (first & 1))
    return sorted(range(n), key=lambda i: (far(i), i))


ORDER = nearest_first(8, 2)


def flipped(n, bit):
    return [(i, i ^ bit) for i in range(n)]


def per_device(
    train_inputs,
    train_outgrads,
    test_inputs,
    test_outgrads,
    train_counts,
    test_counts,
    proj_in,
    proj_out,
    fisher_prior,
):
    n = 8
    length = train_inputs.shape[1]
    counts = (train_counts, test_counts)
    operands = counts + (
        train_inputs, train_outgrads, test_inputs, test_outgrads, proj_in, proj_out
    )
    near = lambda x: lax.ppermute(x, "tensor", flipped(n, 1))
    next_to = lambda x: lax.ppermute(x, "tensor", flipped(n, 2))
    beyond = lambda x: lax.ppermute(x, "tensor", flipped(n, 4))
    (sent0,) = project_rows([(True, 0, (256,))], operands)
    got0 = near(sent0)
    (sent1,) = project_rows([(True, 256, (256,))], operands, (sent0,))
    got1 = near(sent1)
    kept0, sent2 = project_rows([(False, 0, (256,)), (True, 512, (256,))], operands, (sent1,))
    got2 = near(sent2)
    theirs_a, ours_a = halve(1, [(kept0, 0, got0)])
    half_a = next_to(theirs_a)
    kept1, sent3, sent4 = project_rows(
        [(False, 256, (256,)), (True, 768, (128, 128))], operands, (sent2, theirs_a)
    )
    got3 = near(sent3)
    got4 = near(sent4)
    theirs_b, ours_b = halve(1, [(kept1, 0, got1)])
    half_b = next_to(theirs_b)
    send_a, last_a = halve(2, [(ours_a, 0, half_a)], (theirs_b,))
    whole_a = beyond(send_a)
    (kept2,) = project_rows([(False, 512, (256,))], operands, (sent4, send_a))
    theirs_c, ours_c = halve(1, [(kept2, 0, got2)], (whole_a,))
    half_c = next_to(theirs_c)
    send_b, last_b = halve(2, [(ours_b, 0, half_b)], (theirs_c,))
    whole_b = beyond(send_b)
    (kept3,) = project_rows([(False, 768, (256,))], operands, (kept2, send_b))
    theirs_d, ours_d = halve(1, [(kept3, 0, got3)], (send_b,))
    half_d = next_to(theirs_d)
    theirs_e, ours_e = halve(1, [(kept3, 128, got4)], (theirs_d,))
    half_e = next_to(theirs_e)
    send_c, last_c = halve(2, [(ours_c, 0, half_c)], (theirs_e, whole_b))
    whole_c = beyond(send_c)
    send_d, last_d = halve(2, [(ours_d, 0, half_d)], (send_c,))
    whole_d = beyond(send_d)
    send_e, last_e = halve(2, [(ours_e, 0, half_e)], (send_d,))
    whole_e = beyond(send_e)
    square, prior, limit = gram(
        0, length, (last_a, last_b, last_c), (whole_a, whole_b, whole_c), counts, fisher_prior
    )
    grad = gram(768, length, (last_d, last_e), (whole_d, whole_e), before=(square, limit))
    own = lax.all_to_all(grad, "tensor", 0, 0, tiled=True, axis_index_groups=[ORDER])
    other = lax.ppermute(own, "dp", flipped(2, 1))
    per = train_inputs.shape[0]
    state = (8, 8, LANES)
    piece = (8, LANES)
    total = 2 * per
    search, payload = call(begin_kernel, [state, state], (own, prior), [piece])
    swap = lambda x: lax.all_to_all(x, "tensor", 0, 0, tiled=True, axis_index_groups=[ORDER])
    solution, residue, search, payload, grads = call(
        first_kernel,
        [state] * 4 + [(total,) + state],
        (swap(payload), search, own, other, prior),
        [piece],
    )
    for _ in range(ITERS - 3):
        solution, residue, search, payload = call(
            step_kernel,
            [state] * 4,
            (swap(payload), solution, residue, search, grads, prior),
            [piece],
        )
    ours, payload, values = call(
        last_kernel,
        [(3, 8, LANES), state, (2, total, 8, LANES)],
        (swap(payload), solution, residue, search, grads, prior),
        [state, state, state, piece],
    )
    return tuple(
        call(
            end_kernel,
            [(2, total), (2, fisher_prior.shape[0])],
            (swap(payload), ours, values),
        )
    )


def solution(mesh):
    in_specs = (
        P(("parts", "dp"), None, "tensor"),
        P(("parts", "dp"), None, "tensor"),
        P(("parts", "dp"), None, "tensor"),
        P(("parts", "dp"), None, "tensor"),
        P(("parts", "dp")),
        P(("parts", "dp")),
        P(None, "tensor"),
        P(None, "tensor"),
        P(("parts", "tensor"), None),
    )
    out_specs = (P(("parts", "dp"), None), P(("parts", "dp"), "tensor"))
    body = per_device if mesh.shape["tensor"] == 8 and mesh.shape["dp"] == 2 else plain
    return jax.shard_map(
        body, mesh=mesh, in_specs=in_specs, out_specs=out_specs, check_vma=False
    )
```
